256 devices in a mesh: tile: 64 (over x, y, z_lo), frame: 4 (over z_hi, core).
Axes of the slice: x: 4, y: 4, z: 8 (z_hi: 2, z_lo: 4; z = z_hi * 4 + z_lo), core: 2. Of those that a mesh axis runs over, the one named last changes fastest.
Arguments:
- video: float32 [16, 128, 160, 128], P('frame', 'tile'), may hold values from -6 to 6
- norm_gain: float32 [2, 2, 128], replicated, may hold values from 0.1 to 1.9
- space_weight: float32 [2, 3, 3, 128, 128], replicated, may hold values from -0.1875 to 0.1875
- time_weight: float32 [2, 3, 128, 128], replicated, may hold values from -0.3125 to 0.3125
- down_weight: float32 [3, 3, 128, 256], replicated, may hold values from -0.1875 to 0.1875
- attn_gain: float32 [256], replicated, may hold values from 0.1 to 1.9
- w_query: float32 [256, 256], replicated, may hold values from -4 to 4
- w_key: float32 [256, 256], replicated, may hold values from -4 to 4
- w_value: float32 [256, 256], replicated, may hold values from -0.375 to 0.375
- w_out: float32 [256, 256], replicated, may hold values from -0.375 to 0.375
Outputs:
- encoded: float32 [256, 320, 256], P(('frame', 'tile'))
The draws below stay inside these ranges and needn't reach their ends.
All inputs are finite; a program needn't handle non-finite values.
Results may differ from the reference program's by a relative error of at most 0.0003.
Values sent between devices are 32-bit elements; how exact they have to be, the bound alone decides.
A program may use at most 64 MiB of HBM per device.

```python
import jax
import jax.numpy as jnp
from jax import lax

C = 128
C2 = 256
W = 160
FRAMES = 16
H = 128
GROUP = 16
PT = 5
ATOK = 320
KEYS = 5120
FBLOCKS = 256
N_TILE = 64


def draw_w_query(key, part):
    base = jax.random.normal(jax.random.fold_in(key, 11), (C2, C2), jnp.float32)
    base = jnp.clip(base, -4.0, 4.0) * C2 ** (-0.5)
    return base


def draw_w_key(key, part):
    base = jax.random.normal(jax.random.fold_in(key, 12), (C2, C2), jnp.float32)
    base = jnp.clip(base, -4.0, 4.0) * C2 ** (-0.5)
    return base


def block_levels(own_key, extent, split, low, top_value):
    level, own = 1.0, jax.random.fold_in(own_key, 6)
    for axis_at, blocks in split:
        steps = jnp.exp(jax.random.uniform(jax.random.fold_in(own, axis_at), (blocks,), jnp.float32, low / len(split), top_value / len(split)))
        level = level * jnp.repeat(steps, extent[axis_at] // blocks).reshape([-1 if axis == axis_at else 1 for axis in range(len(extent))])
    return level


def bell_draw(rng, extent, spread, limit, shards=(), held_as=jnp.bfloat16):
    level = block_levels(rng, extent, shards, -0.22, 0.18) if shards else 1.0
    values = jax.random.normal(rng, extent, jnp.float32) * spread * level
    return jnp.minimum(jnp.maximum(values, -limit), limit).astype(held_as)


def setup_inputs(seed: int = 0) -> dict:
    splits = jax.random.split(jax.random.key(seed), 11)
    return {
        "video": bell_draw(splits[0], (FRAMES, H, W, C), 1.0, 6.0, ((0, 4), (1, 64)), jnp.float32),
        "norm_gain": jnp.clip(1.0 + 0.18 * jax.random.normal(splits[1], (2, 2, C), jnp.float32), 0.1, 1.9),
        "space_weight": bell_draw(splits[2], (2, 3, 3, C, C), (9 * C) ** -0.5, 0.1875, (), jnp.float32),
        "time_weight": bell_draw(splits[3], (2, 3, C, C), (3 * C) ** -0.5, 0.3125, (), jnp.float32),
        "down_weight": bell_draw(splits[4], (3, 3, C, C2), (9 * C) ** -0.5, 0.1875, (), jnp.float32),
        "attn_gain": jnp.clip(1.0 + 0.18 * jax.random.normal(splits[5], (C2,), jnp.float32), 0.1, 1.9),
        "w_query": draw_w_query(jax.random.fold_in(splits[10], 71), 0),
        "w_key": draw_w_key(jax.random.fold_in(splits[10], 71), 0),
        "w_value": bell_draw(splits[8], (C2, C2), C2 ** -0.5, 0.375, (), jnp.float32),
        "w_out": bell_draw(splits[9], (C2, C2), C2 ** -0.5, 0.375, (), jnp.float32),
    }


highest = lax.Precision.HIGHEST

def norm(values, gain):
    return values * lax.rsqrt(lax.optimization_barrier(jnp.mean(values * values, -1, keepdims=True)) + 1e-06) * gain

def act(values, gain):
    return jax.nn.silu(norm(values, gain))

def conv_space(inputs, kernel):
    return lax.conv_general_dilated(inputs, kernel, (1, 1), ((1, 1), (1, 1)), dimension_numbers=('NHWC', 'HWIO', 'NHWC'), precision=highest)

def conv_time(inputs, kernel):
    padded = jnp.concatenate([inputs[:1], inputs[:1], inputs], 0)
    count = inputs.shape[0]
    total = jnp.einsum('fhwc,cd->fhwd', padded[0:count], kernel[0], precision=highest)
    total = total + jnp.einsum('fhwc,cd->fhwd', padded[1:count + 1], kernel[1], precision=highest)
    total = total + jnp.einsum('fhwc,cd->fhwd', padded[2:count + 2], kernel[2], precision=highest)
    return total

def reference(video, norm_gain, space_weight, time_weight, down_weight, attn_gain, w_query, w_key, w_value, w_out):
    state = video
    for block in range(2):
        mixed = conv_space(act(state, norm_gain[block, 0]), space_weight[block])
        state = state + conv_time(act(mixed, norm_gain[block, 1]), time_weight[block])
    lowered = lax.conv_general_dilated(state, down_weight, (2, 2), ((1, 0), (1, 0)), dimension_numbers=('NHWC', 'HWIO', 'NHWC'), precision=highest)
    flat = lowered.reshape(FRAMES, KEYS, C2)

    def attend(tokens):
        normed = norm(tokens, attn_gain)
        query = jnp.dot(normed, w_query, precision=highest) * C2 ** (-0.5)
        keys = jnp.dot(normed, w_key, precision=highest)
        values = jnp.dot(normed, w_value, precision=highest)
        scores = jnp.dot(query, keys.T, precision=highest)
        weights = jax.nn.softmax(scores, axis=-1)
        mixed = jnp.dot(weights, values, precision=highest)
        return tokens + jnp.dot(mixed, w_out, precision=highest)
    result = lax.map(attend, flat)
    blocks = result.reshape(FRAMES, N_TILE, GROUP, PT, C2).transpose(0, 2, 1, 3, 4)
    return blocks.reshape(FBLOCKS, ATOK, C2)
```

```python
import functools

import jax
import jax.numpy as jnp
from jax import lax
from jax.experimental import pallas as pl
from jax.experimental.pallas import tpu as pltpu
from jax.sharding import PartitionSpec as P

highest = lax.Precision.HIGHEST
MESH = pl.DeviceIdType.MESH
F32 = jnp.float32
BF16 = jnp.bfloat16


def passed_along(shard, axis, by):
    size = lax.axis_size(axis)
    pairs = [(i, i + by) for i in range(size) if 0 <= i + by < size]
    return lax.ppermute(shard, axis, pairs)


def extended(cells, sides, width):
    for axis, dim in sides:
        count = lax.axis_size(axis)
        ends = count - 1
        head = lax.slice_in_dim(cells, 0, width, axis=dim)
        tail = lax.slice_in_dim(cells, cells.shape[dim] - width, cells.shape[dim], axis=dim)
        cells = jnp.concatenate(
            [
                lax.ppermute(tail, axis, [(i, (i + 1) % count) for i in range(ends)]),
                cells,
                lax.ppermute(head, axis, [((i + 1) % count, i) for i in range(ends)]),
            ],
            axis=dim,
        )
    return cells


def norm(values, gain):
    return values * lax.rsqrt(jnp.mean(values * values, -1, keepdims=True) + 1e-06) * gain


def act(values, gain):
    return jax.nn.silu(norm(values, gain))


def conv_rows(inputs, kernel):
    return lax.conv_general_dilated(
        inputs,
        kernel,
        (1, 1),
        ((0, 0), (1, 1)),
        dimension_numbers=("NHWC", "HWIO", "NHWC"),
        precision=highest,
    )


def time_mix(inputs, kernel):
    earlier = passed_along(inputs[-2:], "frame", 1)
    opening = lax.axis_index("frame") == 0
    start = jnp.where(opening, jnp.concatenate([inputs[:1], inputs[:1]], 0), earlier)
    padded = jnp.concatenate([start, inputs], 0)
    count = inputs.shape[0]
    total = jnp.einsum("fhwc,cd->fhwd", padded[0:count], kernel[0], precision=highest)
    total = total + jnp.einsum("fhwc,cd->fhwd", padded[1 : count + 1], kernel[1], precision=highest)
    total = total + jnp.einsum("fhwc,cd->fhwd", padded[2 : count + 2], kernel[2], precision=highest)
    return total


def split(values):
    high = values.astype(BF16)
    return high, (values - high.astype(F32)).astype(BF16)


def three_pass(a, b):
    ah, al = split(a)
    bh, bl = split(b)
    total = jnp.dot(ah, bh, preferred_element_type=F32)
    total = total + jnp.dot(ah, bl, preferred_element_type=F32)
    return total + jnp.dot(al, bh, preferred_element_type=F32)


def dot_f32(a, b, dims=((1,), (0,))):
    return lax.dot_general(a, b, (dims, ((), ())), precision=highest, preferred_element_type=F32)


QT = 128


def attend_kernel(
    z_ref, gain_ref, wq_ref, wk_ref, wv_ref, wo_ref, out_ref,
    keys, query, acc, best, total, normed, part_acc, part_stat, result,
    s1, r1, ss, rs, rets, retr,
):
    tile = lax.axis_index("tile")
    frame = lax.axis_index("frame")
    x, y, z = tile // 16, (tile // 4) % 4, tile % 4
    half, s = z // 2, z % 2
    zh, core = frame // 2, frame % 2

    def dev(x, y, z, core):
        return {"tile": x * 16 + y * 4 + z, "frame": zh * 2 + core}

    up = dev(x, (y + 1) % 4, z, core)
    down = dev(x, (y + 3) % 4, z, core)
    mate = dev(x, y, z + 1 - 2 * s, core)
    sibling = dev(x, y, z, 1 - core)
    sz = 2 * core + s
    crossed = half != core
    idx = y * 4 + sz
    me_q = y * 4 + z

    barrier = pltpu.get_barrier_semaphore()

    def hello(device):
        pl.semaphore_signal(barrier, inc=1, device_id=device, device_id_type=MESH)

    for device in (up, down, mate, sibling):
        hello(device)
    for dx in range(1, 4):
        hello(dev((x + dx) % 4, y, sz, half))

    @pl.when(crossed)
    def _():
        hello(dev(x, y, sz, half))

    for k in range(16):
        sy, ssz, sc = k // 4, 2 * core + (k % 2), (k // 2) % 2

        @pl.when(jnp.logical_not((sy == y) & (ssz == z) & (sc == core)))
        def _():
            hello(dev(x, sy, ssz, sc))

    pl.semaphore_wait(barrier, 22 + 2 * crossed.astype(jnp.int32))

    slot = s * 4 + y
    first = []
    for dx in range(1, 4):
        xt = (x + dx) % 4
        copy = pltpu.make_async_remote_copy(
            src_ref=z_ref.at[xt],
            dst_ref=keys.at[slot, pl.ds(pl.multiple_of(x * 80, 80), 80)],
            send_sem=s1.at[dx],
            recv_sem=r1.at[dx],
            device_id=dev(xt, y, sz, half),
            device_id_type=MESH,
        )
        copy.start()
        first.append(copy)
    cross = pltpu.make_async_remote_copy(
        src_ref=z_ref.at[x],
        dst_ref=keys.at[slot, pl.ds(pl.multiple_of(x * 80, 80), 80)],
        send_sem=s1.at[0],
        recv_sem=r1.at[0],
        device_id=dev(x, y, sz, half),
        device_id_type=MESH,
    )

    @pl.when(crossed)
    def _():
        cross.start()

    @pl.when(jnp.logical_not(crossed))
    def _():
        keys[slot, pl.ds(pl.multiple_of(x * 80, 80), 80), :] = z_ref[x]

    for copy in first:
        copy.wait_recv()

    @pl.when(crossed)
    def _():
        cross.wait_recv()

    slot_up = s * 4 + (y + 1) % 4
    slot_down = s * 4 + (y + 3) % 4
    slot_far = s * 4 + (y + 2) % 4
    other = (1 - s) * 4
    mate_own, mate_up = other + y, other + (y + 1) % 4
    mate_down, mate_far = other + (y + 3) % 4, other + (y + 2) % 4
    lo, hi = pl.ds(0, 160), pl.ds(160, 160)

    def remote(src, dst, device, i):
        return pltpu.make_async_remote_copy(
            src_ref=src, dst_ref=dst, send_sem=ss.at[i], recv_sem=rs.at[i],
            device_id=device, device_id_type=MESH,
        )

    def push(i, block, device, rows=None):
        ref = keys.at[block] if rows is None else keys.at[block, rows]
        copy = remote(ref, ref, device, i)
        copy.start()
        return copy

    def landed(i, block, device, rows=None):
        ref = keys.at[block] if rows is None else keys.at[block, rows]
        remote(ref, ref, device, i).wait_recv()

    sent = [push(0, slot, up), push(1, slot, down), push(2, slot, mate)]

    gain = gain_ref[...]
    own = norm(keys[slot], gain)
    projected = dot_f32(own, wq_ref[...]) * (256.0 ** -0.5)
    query[0] = dot_f32(projected, wk_ref[...], ((1,), (1,)))
    q_copy = remote(query.at[0], query.at[1], sibling, 8)
    q_copy.start()
    sent.append(q_copy)

    best[...] = jnp.full_like(best, -jnp.inf)
    total[...] = jnp.zeros_like(total)
    acc[...] = jnp.zeros_like(acc)

    def attend(block, which):
        normed[...] = norm(keys[block], gain)

        def tile_step(t, _):
            rows = pl.ds(pl.multiple_of(t * 64, 64), 64)
            k = normed[...]
            scores = dot_f32(query[which, rows, :], k, ((1,), (1,)))
            old = best[which, rows, :]
            new = jnp.maximum(old, jnp.max(scores, axis=1, keepdims=True))
            factor = jnp.exp(old - new)
            weights = jnp.exp(scores - new)
            total[which, rows, :] = total[which, rows, :] * factor + jnp.sum(weights, axis=1, keepdims=True)
            best[which, rows, :] = new
            acc[which, rows, :] = acc[which, rows, :] * factor + three_pass(weights, k)
            return 0

        lax.fori_loop(0, 5, tile_step, 0)

    def attend_both(block):
        attend(block, 1)
        attend(block, 0)

    attend(slot, 0)
    q_copy.wait_recv()
    attend(slot, 1)
    landed(0, slot_down, up)
    sent.append(push(5, slot_down, up, lo))
    landed(1, slot_up, down)
    sent.append(push(6, slot_up, down, hi))
    landed(2, mate_own, mate)
    sent.append(push(3, mate_own, up))
    sent.append(push(4, mate_own, down))
    attend_both(slot_down)
    attend_both(slot_up)
    landed(5, slot_far, up, lo)
    landed(6, slot_far, down, hi)
    sent.append(push(7, slot_far, mate))
    attend_both(mate_own)
    attend_both(slot_far)
    landed(3, mate_down, up)
    attend_both(mate_down)
    landed(4, mate_up, down)
    attend_both(mate_up)
    landed(7, mate_far, mate)
    attend(mate_far, 1)
    part_stat[0, 0, :, :] = jnp.broadcast_to(best[1], (320, 128))
    part_stat[0, 1, :, :] = jnp.broadcast_to(total[1], (320, 128))
    merge = [
        remote(acc.at[1], part_acc, sibling, 9),
        remote(part_stat.at[0], part_stat.at[1], sibling, 10),
    ]
    for copy in merge:
        copy.start()
    attend(mate_far, 0)
    for copy in merge:
        copy.wait_recv()
    sent.extend(merge)
    other_best = part_stat[1, 0, :, 0:1]
    other_total = part_stat[1, 1, :, 0:1]
    top = jnp.maximum(best[0], other_best)
    mine_f = jnp.exp(best[0] - top)
    other_f = jnp.exp(other_best - top)
    whole = total[0] * mine_f + other_total * other_f
    mixed = (acc[0] * mine_f + part_acc[...] * other_f) / whole
    value = dot_f32(mixed, wv_ref[...])
    y_out = keys[slot] + dot_f32(value, wo_ref[...])
    for q in range(16):
        for b in range(4):
            start = b * 80 + q * 5
            result[q, b] = y_out[start : start + 5]

    backs = []
    for k in range(16):
        q = (me_q + k) % 16
        copy = pltpu.make_async_remote_copy(
            src_ref=result.at[q],
            dst_ref=out_ref.at[:, idx],
            send_sem=rets.at[k],
            recv_sem=retr.at[idx],
            device_id=dev(x, q // 4, q % 4, half),
            device_id_type=MESH,
        )
        backs.append(copy)
        if k > 0:
            copy.start()

    @pl.when(crossed)
    def _():
        backs[0].start()

    @pl.when(jnp.logical_not(crossed))
    def _():
        out_ref[:, pl.ds(idx, 1), :, :] = result[me_q][:, None]

    for copy in first:
        copy.wait_send()

    @pl.when(crossed)
    def _():
        cross.wait_send()
        backs[0].wait_send()

    for copy in sent:
        copy.wait_send()
    for k in range(16):
        if k > 0:
            backs[k].wait_send()
        sy, ssz, sc = k // 4, 2 * core + (k % 2), (k // 2) % 2

        @pl.when(jnp.logical_not((sy == y) & (ssz == z) & (sc == core)))
        def _():
            pltpu.make_async_remote_copy(
                src_ref=result.at[0],
                dst_ref=out_ref.at[:, k],
                send_sem=rets.at[k],
                recv_sem=retr.at[k],
                device_id=sibling,
                device_id_type=MESH,
            ).wait_recv()


def attend_all(lowered, attn_gain, w_query, w_key, w_value, w_out):
    vmem = pl.BlockSpec(memory_space=pltpu.VMEM)
    dma = pltpu.SemaphoreType.DMA
    out = pl.pallas_call(
        attend_kernel,
        out_shape=jax.ShapeDtypeStruct((4, 16, 5, 256), F32),
        in_specs=[vmem] * 6,
        out_specs=vmem,
        scratch_shapes=[
            pltpu.VMEM((8, 320, 256), F32),
            pltpu.VMEM((2, 320, 256), F32),
            pltpu.VMEM((2, 320, 256), F32),
            pltpu.VMEM((2, 320, 1), F32),
            pltpu.VMEM((2, 320, 1), F32),
            pltpu.VMEM((320, 256), F32),
            pltpu.VMEM((320, 256), F32),
            pltpu.VMEM((2, 2, 320, 128), F32),
            pltpu.VMEM((16, 4, 5, 256), F32),
            dma((4,)), dma((4,)), dma((11,)), dma((11,)), dma((16,)), dma((16,)),
        ],
        compiler_params=pltpu.CompilerParams(
            collective_id=1, has_side_effects=True, vmem_limit_bytes=40 * 2**20
        ),
        name="attend",
    )(lowered, attn_gain.reshape(1, 256), w_query, w_key, w_value, w_out)
    return out.reshape(1, 320, 256)


def local(
    video,
    norm_gain,
    space_weight,
    time_weight,
    down_weight,
    attn_gain,
    w_query,
    w_key,
    w_value,
    w_out,
):
    state = video
    for block in range(2):
        wide = extended(act(state, norm_gain[block, 0]), (("tile", 1),), 1)
        mixed = conv_rows(wide, space_weight[block])
        state = state + time_mix(act(mixed, norm_gain[block, 1]), time_weight[block])
    upper = passed_along(state[:, -1:], "tile", 1)
    stacked = jnp.concatenate([upper, state], 1)
    lowered = lax.conv_general_dilated(
        stacked,
        down_weight,
        (2, 2),
        ((0, 0), (1, 0)),
        dimension_numbers=("NHWC", "HWIO", "NHWC"),
        precision=highest,
    )
    lowered = lowered.reshape(4, 80, 256)
    return attend_all(lowered, attn_gain, w_query, w_key, w_value, w_out)


def solution(mesh):
    in_specs = (P("frame", "tile", None, None), P(), P(), P(), P(), P(), P(), P(), P(), P())
    out_specs = P(("frame", "tile"), None, None)
    return jax.shard_map(local, mesh=mesh, in_specs=in_specs, out_specs=out_specs, check_vma=False)
```

```python
import functools

import jax
import jax.numpy as jnp
from jax import lax
from jax.experimental import pallas as pl
from jax.experimental.pallas import tpu as pltpu
from jax.sharding import PartitionSpec as P

highest = lax.Precision.HIGHEST
MESH = pl.DeviceIdType.MESH
F32 = jnp.float32
BF16 = jnp.bfloat16


def norm(values, gain):
    return values * lax.rsqrt(jnp.mean(values * values, -1, keepdims=True) + 1e-06) * gain


def split(values):
    high = values.astype(BF16)
    return high, (values - high.astype(F32)).astype(BF16)


LEFT, RIGHT = 7, 48


def act(values, gain):
    scaled = values * lax.rsqrt(jnp.mean(values * values, -1, keepdims=True) + 1e-06) * gain
    return scaled / (1.0 + jnp.exp(-scaled))


def conv_kernel(
    video_ref, gain_ref, space_ref, time_ref, down_ref, out_ref,
    state, padded, ext, ext_in, cols, cols_in, corners, corners_in,
    late, late_in, u_hi, u_lo, a_hi, a_lo, d_hi, d_lo, w_space, w_time, w_hi, w_lo,
    send_sems, recv_sems,
):
    tile = lax.axis_index("tile")
    frame = lax.axis_index("frame")
    k, z = tile // 4, tile % 4
    has_up, has_down = k > 0, k < 15
    has_left, has_right = z > 0, z < 3

    def dev(k, z, frame=frame):
        return {"tile": k * 4 + z, "frame": frame}

    def when(cond, fn):
        if cond is None:
            fn()
        else:
            pl.when(cond)(fn)

    ids = {}
    sent = []

    def message(name, src, dst, device):
        i = ids.setdefault(name, len(ids))
        return pltpu.make_async_remote_copy(
            src_ref=src, dst_ref=dst, send_sem=send_sems.at[i], recv_sem=recv_sems.at[i],
            device_id=device, device_id_type=MESH,
        )

    def start(name, src, dst, device, cond=None):
        copy = message(name, src, dst, device)
        when(cond, copy.start)
        sent.append((copy, cond))

    def arrived(name, ref, cond=None):
        copy = message(name, ref, ref, dev(k, (z + 1) % 4))
        when(cond, copy.wait_recv)

    for b in range(3):
        padded[b, :, :, 0:8, :] = jnp.zeros((4, 10, 8, 128), F32)
        padded[b, :, :, 48:56, :] = jnp.zeros((4, 10, 8, 128), F32)

        @pl.when(jnp.logical_not(has_up))
        def _():
            padded[b, :, 0, :, :] = jnp.zeros((4, 56, 128), F32)

        @pl.when(jnp.logical_not(has_down))
        def _():
            padded[b, :, 9, :, :] = jnp.zeros((4, 56, 128), F32)

    barrier = pltpu.get_barrier_semaphore()

    def hello(device, cond=None):
        when(cond, lambda: pl.semaphore_signal(barrier, inc=1, device_id=device, device_id_type=MESH))

    sides = ((-1, has_up), (1, has_down))
    flanks = ((-1, has_left), (1, has_right))
    for dz in range(1, 4):
        hello(dev(k, (z + dz) % 4))
    for dk, ok in sides:
        hello(dev((k + dk) % 16, z), ok)
        for dz, fine in flanks:
            hello(dev((k + dk) % 16, (z + dz) % 4), ok & fine)
    hello(dev(k, z, (frame + 3) % 4), frame > 0)
    count = 3 + (frame < 3).astype(jnp.int32)
    across = 1 + has_left.astype(jnp.int32) + has_right.astype(jnp.int32)
    count = count + (has_up.astype(jnp.int32) + has_down.astype(jnp.int32)) * across
    pl.semaphore_wait(barrier, count)

    order = (2, 3, 0, 1)
    for part in range(4):
        for fr in range(4):
            if part == 0:
                ext[part, fr, 0:2] = jnp.zeros((2, 1, 128), F32)
            else:
                ext[part, fr, 0:2] = video_ref[fr, :, 40 * part - 1 : 40 * part, :]
            if part == 3:
                ext[part, fr, 2:4] = jnp.zeros((2, 1, 128), F32)
            else:
                ext[part, fr, 2:4] = video_ref[fr, :, 40 * part + 40 : 40 * part + 41, :]

    def band(part):
        return pl.ds(pl.multiple_of(part * 40, 8), 40)

    for dz in (2, 1, 3):
        part = (z + dz) % 4
        start(("ext", dz), ext.at[part], ext_in.at[z], dev(k, part))
    for fr in order:
        for dz in (2, 1, 3):
            part = (z + dz) % 4
            start(("band", fr, dz), video_ref.at[fr, :, band(part), :], state.at[fr, pl.ds(z * 2, 2)], dev(k, part))
    ext_in[z] = ext[z]
    for fr in range(4):
        state[fr, pl.ds(z * 2, 2)] = video_ref[fr, :, band(z), :]

    for b in range(2):
        for tap in range(9):
            rows = slice(tap * 128, tap * 128 + 128)
            high, low = split(space_ref[b, rows, :])
            w_space[b, rows, 0:128] = high
            w_space[b, rows, 128:256] = low
        high, low = split(time_ref[b])
        w_time[b, :, 0:128] = high
        w_time[b, :, 128:256] = low
    for tap in range(9):
        rows = slice(tap * 128, tap * 128 + 128)
        high, low = split(down_ref[rows, :])
        w_hi[rows, :] = high
        w_lo[rows, :] = low

    def two_part(high, low, weight):
        both = jnp.dot(high, weight, preferred_element_type=F32)
        rest = jnp.dot(low, weight[:, 0:128], preferred_element_type=F32)
        return both[:, 0:128] + both[:, 128:256] + rest

    inner = pl.ds(8, 40)

    def send_rows(b, f0, nf, width, both=True):
        f = pl.ds(f0, nf)
        start(("row", b, f0, 1), padded.at[b, f, 8, width, :], padded.at[b, f, 0, width, :], dev((k + 1) % 16, z), has_down)
        if both:
            start(("row", b, f0, -1), padded.at[b, f, 1, width, :], padded.at[b, f, 9, width, :], dev((k + 15) % 16, z), has_up)

    def rows_arrived(b, f0, nf, width, both=True):
        f = pl.ds(f0, nf)
        arrived(("row", b, f0, 1), padded.at[b, f, 0, width, :], has_up)
        if both:
            arrived(("row", b, f0, -1), padded.at[b, f, 9, width, :], has_down)

    def directions(both):
        return ((1, 1), (1, -1), (-1, 1), (-1, -1)) if both else ((1, 1),)

    def send_edges(b, f0, nf, both=True):
        f = pl.ds(f0, nf)
        for fr in range(f0, f0 + nf):
            cols[b - 1, 1, fr] = padded[b, fr, 1:9, 47:48, :]
            if both:
                cols[b - 1, 0, fr] = padded[b, fr, 1:9, 8:9, :]
            for dk, dz in directions(both):
                row, col = 8 if dk > 0 else 1, 47 if dz > 0 else 8
                corners[b - 1, (dk > 0) * 2 + (dz > 0), fr] = padded[b, fr, row, col : col + 1, :]
        start(("col", b, f0, 1), cols.at[b - 1, 1, f], cols_in.at[b - 1, 1, f], dev(k, (z + 1) % 4), has_right)
        if both:
            start(("col", b, f0, -1), cols.at[b - 1, 0, f], cols_in.at[b - 1, 0, f], dev(k, (z + 3) % 4), has_left)
        for dk, dz in directions(both):
            c = (dk > 0) * 2 + (dz > 0)
            ok = (has_down if dk > 0 else has_up) & (has_right if dz > 0 else has_left)
            start(
                ("corner", b, f0, dk, dz), corners.at[b - 1, c, f], corners_in.at[b - 1, c, f],
                dev((k + dk) % 16, (z + dz) % 4), ok,
            )

    def edges_arrived(b, f0, nf, both=True):
        f = pl.ds(f0, nf)
        rows_arrived(b, f0, nf, inner, both)
        arrived(("col", b, f0, 1), cols_in.at[b - 1, 1, f], has_left)
        if both:
            arrived(("col", b, f0, -1), cols_in.at[b - 1, 0, f], has_right)

        @pl.when(has_left)
        def _():
            for fr in range(f0, f0 + nf):
                padded[b, fr, 1:9, LEFT : LEFT + 1, :] = cols_in[b - 1, 1, fr]

        if both:
            @pl.when(has_right)
            def _():
                for fr in range(f0, f0 + nf):
                    padded[b, fr, 1:9, RIGHT : RIGHT + 1, :] = cols_in[b - 1, 0, fr]

        for dk, dz in directions(both):
            c = (dk > 0) * 2 + (dz > 0)
            ok = (has_up if dk > 0 else has_down) & (has_left if dz > 0 else has_right)
            arrived(("corner", b, f0, dk, dz), corners_in.at[b - 1, c, f], ok)

            @pl.when(ok)
            def _():
                row, col = 0 if dk > 0 else 9, LEFT if dz > 0 else RIGHT
                for fr in range(f0, f0 + nf):
                    padded[b, fr, row, col : col + 1, :] = corners_in[b - 1, c, fr]

    def conv(b, fr):
        at = fr % 2
        for dx in range(3):
            window = padded[b, fr, :, LEFT + dx : LEFT + dx + 40, :]
            for dy in range(3):
                lanes = slice((dy * 3 + dx) * 128, (dy * 3 + dx) * 128 + 128)
                high, low = split(window[dy : dy + 8].reshape(320, 128))
                a_hi[at, :, lanes] = high
                a_lo[at, :, lanes] = low
        mixed = two_part(a_hi[at], a_lo[at], w_space[b])
        u = act(mixed, gain_ref[b, 1:2, :])
        put(fr, u)
        if fr >= 2:
            late[b, fr - 2] = u
            start(
                ("late", b, fr), late.at[b, fr - 2], late_in.at[b, fr - 2],
                dev(k, z, (frame + 1) % 4), frame < 3,
            )

    def put(fr, u):
        lanes = slice((fr + 2) * 128, (fr + 3) * 128)
        u_hi[:, lanes], u_lo[:, lanes] = split(u)

    def earlier(b):
        for fr in (2, 3):
            arrived(("late", b, fr), late_in.at[b, fr - 2], frame > 0)

        @pl.when(frame > 0)
        def _():
            put(-2, late_in[b, 0])
            put(-1, late_in[b, 1])

        @pl.when(frame == 0)
        def _():
            for parts in (u_hi, u_lo):
                parts[:, 0:128] = parts[:, 256:384]
                parts[:, 128:256] = parts[:, 256:384]

    def mix(b, fr):
        lanes = slice(fr * 128, fr * 128 + 384)
        return state[fr].reshape(320, 128) + two_part(u_hi[:, lanes], u_lo[:, lanes], w_time[b])

    for dz in range(1, 4):
        arrived(("ext", dz), ext_in.at[(z + dz) % 4])
    gain = gain_ref[0, 0:1, :]
    for fr in order:
        for dz in range(1, 4):
            arrived(("band", fr, dz), state.at[fr, pl.ds(((z + dz) % 4) * 2, 2)])
        padded[0, fr, 1:9, 8:48, :] = act(state[fr].reshape(320, 128), gain).reshape(8, 40, 128)
        for src in range(4):
            fringe = act(ext_in[src, fr], gain)
            rows = slice(1 + 2 * src, 3 + 2 * src)

            @pl.when(has_left)
            def _():
                padded[0, fr, rows, LEFT : LEFT + 1, :] = fringe[0:2]

            @pl.when(has_right)
            def _():
                padded[0, fr, rows, RIGHT : RIGHT + 1, :] = fringe[2:4]
        send_rows(0, fr, 1, slice(None))
    for fr in order:
        rows_arrived(0, fr, 1, slice(None))
        conv(0, fr)

    gain = gain_ref[1, 0:1, :]
    for f0 in (2, 0):
        if f0 == 0:
            earlier(0)
        for fr in (f0, f0 + 1):
            x = mix(0, fr)
            padded[1, fr, 1:9, 8:48, :] = act(x, gain).reshape(8, 40, 128)
            late_x = x.reshape(8, 40, 128)
            state[fr] = late_x
        send_rows(1, f0, 2, inner)
        send_edges(1, f0, 2)
    for f0 in (2, 0):
        edges_arrived(1, f0, 2)
        for fr in (f0, f0 + 1):
            conv(1, fr)
    for f0 in (2, 0):
        if f0 == 0:
            earlier(1)
        for fr in (f0, f0 + 1):
            padded[2, fr, 1:9, 8:48, :] = mix(1, fr).reshape(8, 40, 128)
        send_rows(2, f0, 2, inner, False)
        send_edges(2, f0, 2, False)

    for f0 in (2, 0):
        edges_arrived(2, f0, 2, False)
        for fr in (f0, f0 + 1):
            for row in range(4):
                at = slice((fr - f0) * 96 + row * 24, (fr - f0) * 96 + row * 24 + 24)
                for dy in range(3):
                    for dx in range(3):
                        taken = padded[2, fr, 2 * row + dy, pl.ds(LEFT + dx, 24, stride=2), :]
                        lanes = slice((dy * 3 + dx) * 128, (dy * 3 + dx) * 128 + 128)
                        high = taken.astype(BF16).astype(F32)
                        d_hi[at, lanes] = high
                        d_lo[at, lanes] = taken - high
        high, low = d_hi[...].astype(BF16), d_lo[...].astype(BF16)
        lowered = jnp.dot(high, w_hi[...], preferred_element_type=F32)
        lowered = lowered + jnp.dot(high, w_lo[...], preferred_element_type=F32)
        lowered = lowered + jnp.dot(low, w_hi[...], preferred_element_type=F32)
        for fr in (f0, f0 + 1):
            for row in range(4):
                for part in range(4):
                    at = (fr - f0) * 96 + row * 24 + part * 5
                    out_ref[fr, part * 20 + row * 5 : part * 20 + row * 5 + 5, :] = lowered[at : at + 5]

    for copy, cond in sent:
        when(cond, copy.wait_send)


def conv_all(video, norm_gain, space_weight, time_weight, down_weight):
    vmem = pl.BlockSpec(memory_space=pltpu.VMEM)
    dma = pltpu.SemaphoreType.DMA
    return pl.pallas_call(
        conv_kernel,
        out_shape=jax.ShapeDtypeStruct((4, 80, 256), F32),
        in_specs=[vmem] * 5,
        out_specs=vmem,
        scratch_shapes=[
            pltpu.VMEM((4, 8, 40, 128), F32),
            pltpu.VMEM((3, 4, 10, 56, 128), F32),
            pltpu.VMEM((4, 4, 4, 1, 128), F32),
            pltpu.VMEM((4, 4, 4, 1, 128), F32),
            pltpu.VMEM((2, 2, 4, 8, 1, 128), F32),
            pltpu.VMEM((2, 2, 4, 8, 1, 128), F32),
            pltpu.VMEM((2, 4, 4, 1, 128), F32),
            pltpu.VMEM((2, 4, 4, 1, 128), F32),
            pltpu.VMEM((2, 2, 320, 128), F32),
            pltpu.VMEM((2, 2, 320, 128), F32),
            pltpu.VMEM((320, 768), BF16),
            pltpu.VMEM((320, 768), BF16),
            pltpu.VMEM((2, 320, 1152), BF16),
            pltpu.VMEM((2, 320, 1152), BF16),
            pltpu.VMEM((192, 1152), F32),
            pltpu.VMEM((192, 1152), F32),
            pltpu.VMEM((2, 1152, 256), BF16),
            pltpu.VMEM((2, 384, 256), BF16),
            pltpu.VMEM((1152, 256), BF16),
            pltpu.VMEM((1152, 256), BF16),
            dma((64,)), dma((64,)),
        ],
        compiler_params=pltpu.CompilerParams(
            collective_id=2, has_side_effects=True, vmem_limit_bytes=48 * 2**20
        ),
        name="blocks",
    )(
        video, norm_gain, space_weight.reshape(2, 1152, 128), time_weight.reshape(2, 384, 128),
        down_weight.reshape(1152, 256),
    )


def three_pass(a, b):
    ah, al = split(a)
    bh, bl = split(b)
    total = jnp.dot(ah, bh, preferred_element_type=F32)
    total = total + jnp.dot(ah, bl, preferred_element_type=F32)
    return total + jnp.dot(al, bh, preferred_element_type=F32)


def dot_f32(a, b, dims=((1,), (0,))):
    return lax.dot_general(a, b, (dims, ((), ())), precision=highest, preferred_element_type=F32)


def attend_kernel(
    z_ref, gain_ref, wq_ref, wk_ref, wv_ref, wo_ref, out_ref,
    keys, query, acc, best, total, normed, part_acc, part_stat, result,
    s1, r1, ss, rs, rets, retr,
):
    tile = lax.axis_index("tile")
    frame = lax.axis_index("frame")
    x, y, z = tile // 16, (tile // 4) % 4, tile % 4
    half, s = z // 2, z % 2
    zh, core = frame // 2, frame % 2

    def dev(x, y, z, core):
        return {"tile": x * 16 + y * 4 + z, "frame": zh * 2 + core}

    up = dev(x, (y + 1) % 4, z, core)
    down = dev(x, (y + 3) % 4, z, core)
    mate = dev(x, y, z + 1 - 2 * s, core)
    sibling = dev(x, y, z, 1 - core)
    sz = 2 * core + s
    crossed = half != core

    barrier = pltpu.get_barrier_semaphore()

    def hello(device):
        pl.semaphore_signal(barrier, inc=1, device_id=device, device_id_type=MESH)

    for device in (up, down, mate, sibling):
        hello(device)
    for dx in range(1, 4):
        hello(dev((x + dx) % 4, y, sz, half))

    @pl.when(crossed)
    def _():
        hello(dev(x, y, sz, half))

    from_z, from_core = 2 * core + y % 2, y // 2
    expected = 7 + crossed.astype(jnp.int32)
    for j in range(4):
        @pl.when(jnp.logical_not((j == y) & (from_z == z) & (from_core == core)))
        def _():
            hello(dev(x, j, from_z, from_core))

        expected = expected + jnp.logical_not((sz == y) & (z == j) & (half == core)).astype(jnp.int32)
    pl.semaphore_wait(barrier, expected)

    slot = s * 4 + y
    first = []
    for dx in range(1, 4):
        xt = (x + dx) % 4
        copy = pltpu.make_async_remote_copy(
            src_ref=z_ref.at[xt],
            dst_ref=keys.at[slot, pl.ds(pl.multiple_of(x * 80, 80), 80)],
            send_sem=s1.at[dx],
            recv_sem=r1.at[dx],
            device_id=dev(xt, y, sz, half),
            device_id_type=MESH,
        )
        copy.start()
        first.append(copy)
    cross = pltpu.make_async_remote_copy(
        src_ref=z_ref.at[x],
        dst_ref=keys.at[slot, pl.ds(pl.multiple_of(x * 80, 80), 80)],
        send_sem=s1.at[0],
        recv_sem=r1.at[0],
        device_id=dev(x, y, sz, half),
        device_id_type=MESH,
    )

    @pl.when(crossed)
    def _():
        cross.start()

    @pl.when(jnp.logical_not(crossed))
    def _():
        keys[slot, pl.ds(pl.multiple_of(x * 80, 80), 80), :] = z_ref[x]

    for copy in first:
        copy.wait_recv()

    @pl.when(crossed)
    def _():
        cross.wait_recv()

    slot_up = s * 4 + (y + 1) % 4
    slot_down = s * 4 + (y + 3) % 4
    slot_far = s * 4 + (y + 2) % 4
    other = (1 - s) * 4
    mate_own, mate_up = other + y, other + (y + 1) % 4
    mate_down, mate_far = other + (y + 3) % 4, other + (y + 2) % 4
    lo, hi = pl.ds(0, 160), pl.ds(160, 160)

    def remote(src, dst, device, i):
        return pltpu.make_async_remote_copy(
            src_ref=src, dst_ref=dst, send_sem=ss.at[i], recv_sem=rs.at[i],
            device_id=device, device_id_type=MESH,
        )

    def push(i, block, device, rows=None):
        ref = keys.at[block] if rows is None else keys.at[block, rows]
        copy = remote(ref, ref, device, i)
        copy.start()
        return copy

    def landed(i, block, device, rows=None):
        ref = keys.at[block] if rows is None else keys.at[block, rows]
        remote(ref, ref, device, i).wait_recv()

    sent = [push(0, slot, up), push(1, slot, down), push(2, slot, mate)]

    gain = gain_ref[...]
    own = norm(keys[slot], gain)
    projected = dot_f32(own, wq_ref[...]) * (256.0 ** -0.5)
    query[0] = dot_f32(projected, wk_ref[...], ((1,), (1,)))
    q_copy = remote(query.at[0], query.at[1], sibling, 8)
    q_copy.start()
    sent.append(q_copy)

    best[...] = jnp.full_like(best, -jnp.inf)
    total[...] = jnp.zeros_like(total)
    acc[...] = jnp.zeros_like(acc)

    def attend(block, which):
        normed[...] = norm(keys[block], gain)

        k = normed[...]
        scores = dot_f32(query[which], k, ((1,), (1,)))
        old = best[which]
        new = jnp.maximum(old, jnp.max(scores, axis=1, keepdims=True))
        factor = jnp.exp(old - new)
        weights = jnp.exp(scores - new)
        total[which] = total[which] * factor + jnp.sum(weights, axis=1, keepdims=True)
        best[which] = new
        acc[which] = acc[which] * factor + three_pass(weights, k)

    def attend_both(block):
        attend(block, 1)
        attend(block, 0)

    attend(slot, 0)
    q_copy.wait_recv()
    attend(slot, 1)
    landed(0, slot_down, up)
    sent.append(push(5, slot_down, up, lo))
    landed(1, slot_up, down)
    sent.append(push(6, slot_up, down, hi))
    landed(2, mate_own, mate)
    sent.append(push(3, mate_own, up))
    sent.append(push(4, mate_own, down))
    attend_both(slot_down)
    attend_both(slot_up)
    landed(5, slot_far, up, lo)
    landed(6, slot_far, down, hi)
    sent.append(push(7, slot_far, mate))
    attend_both(mate_own)
    attend_both(slot_far)
    landed(3, mate_down, up)
    attend_both(mate_down)
    landed(4, mate_up, down)
    attend_both(mate_up)
    landed(7, mate_far, mate)
    attend(mate_far, 1)
    part_stat[0, 0, :, :] = jnp.broadcast_to(best[1], (320, 128))
    part_stat[0, 1, :, :] = jnp.broadcast_to(total[1], (320, 128))
    merge = [
        remote(acc.at[1], part_acc, sibling, 9),
        remote(part_stat.at[0], part_stat.at[1], sibling, 10),
    ]
    for copy in merge:
        copy.start()
    attend(mate_far, 0)
    for copy in merge:
        copy.wait_recv()
    sent.extend(merge)
    other_best = part_stat[1, 0, :, 0:1]
    other_total = part_stat[1, 1, :, 0:1]
    top = jnp.maximum(best[0], other_best)
    mine_f = jnp.exp(best[0] - top)
    other_f = jnp.exp(other_best - top)
    whole = total[0] * mine_f + other_total * other_f
    mixed = (acc[0] * mine_f + part_acc[...] * other_f) / whole
    value = dot_f32(mixed, wv_ref[...])
    y_out = keys[slot] + dot_f32(value, wo_ref[...])
    for part in range(4):
        for b in range(4):
            start = b * 80 + part * 20
            result[part, b] = y_out[start : start + 20]

    backs = []
    for part in range(4):
        copy = pltpu.make_async_remote_copy(
            src_ref=result.at[part],
            dst_ref=out_ref.at[:, y],
            send_sem=rets.at[part],
            recv_sem=retr.at[y],
            device_id=dev(x, sz, part, half),
            device_id_type=MESH,
        )
        stays = (sz == y) & (z == part) & (half == core)
        backs.append((copy, stays))

        @pl.when(jnp.logical_not(stays))
        def _():
            copy.start()

        @pl.when(stays)
        def _():
            out_ref[:, pl.ds(y, 1), :, :] = result[part][:, None]

    for copy in first:
        copy.wait_send()

    @pl.when(crossed)
    def _():
        cross.wait_send()

    for copy in sent:
        copy.wait_send()
    for copy, stays in backs:
        @pl.when(jnp.logical_not(stays))
        def _():
            copy.wait_send()
    for sy in range(4):
        here = (sy == y) & (z == 2 * core + y % 2) & (core == y // 2)

        @pl.when(jnp.logical_not(here))
        def _():
            pltpu.make_async_remote_copy(
                src_ref=result.at[0],
                dst_ref=out_ref.at[:, sy],
                send_sem=rets.at[0],
                recv_sem=retr.at[sy],
                device_id=sibling,
                device_id_type=MESH,
            ).wait_recv()


def attend_all(lowered, attn_gain, w_query, w_key, w_value, w_out):
    vmem = pl.BlockSpec(memory_space=pltpu.VMEM)
    dma = pltpu.SemaphoreType.DMA
    out = pl.pallas_call(
        attend_kernel,
        out_shape=jax.ShapeDtypeStruct((4, 4, 20, 256), F32),
        in_specs=[vmem] * 6,
        out_specs=vmem,
        scratch_shapes=[
            pltpu.VMEM((8, 320, 256), F32),
            pltpu.VMEM((2, 320, 256), F32),
            pltpu.VMEM((2, 320, 256), F32),
            pltpu.VMEM((2, 320, 1), F32),
            pltpu.VMEM((2, 320, 1), F32),
            pltpu.VMEM((320, 256), F32),
            pltpu.VMEM((320, 256), F32),
            pltpu.VMEM((2, 2, 320, 128), F32),
            pltpu.VMEM((4, 4, 20, 256), F32),
            dma((4,)), dma((4,)), dma((11,)), dma((11,)), dma((4,)), dma((4,)),
        ],
        compiler_params=pltpu.CompilerParams(
            collective_id=1, has_side_effects=True, vmem_limit_bytes=40 * 2**20
        ),
        name="attend",
    )(lowered, attn_gain.reshape(1, 256), w_query, w_key, w_value, w_out)
    return out.reshape(1, 320, 256)


def local(
    video,
    norm_gain,
    space_weight,
    time_weight,
    down_weight,
    attn_gain,
    w_query,
    w_key,
    w_value,
    w_out,
):
    lowered = conv_all(video, norm_gain, space_weight, time_weight, down_weight)
    return attend_all(lowered, attn_gain, w_query, w_key, w_value, w_out)


def solution(mesh):
    in_specs = (P("frame", "tile", None, None), P(), P(), P(), P(), P(), P(), P(), P(), P())
    out_specs = P(("frame", "tile"), None, None)
    return jax.shard_map(local, mesh=mesh, in_specs=in_specs, out_specs=out_specs, check_vma=False)
```

```python
import jax
import jax.numpy as jnp
from jax import lax
from jax.experimental import pallas as pl
from jax.experimental.pallas import tpu as pltpu
from jax.sharding import PartitionSpec as P

highest = lax.Precision.HIGHEST
MESH = pl.DeviceIdType.MESH
F32 = jnp.float32
BF16 = jnp.bfloat16


def norm(values, gain):
    return values * lax.rsqrt(jnp.mean(values * values, -1, keepdims=True) + 1e-06) * gain


def split(values):
    high = values.astype(BF16)
    return high, (values - high.astype(F32)).astype(BF16)


LEFT, RIGHT = 7, 48


def act(values, gain):
    scaled = values * lax.rsqrt(jnp.mean(values * values, -1, keepdims=True) + 1e-06) * gain
    return scaled / (1.0 + jnp.exp(-scaled))


def conv_part(
    video_hbm, space_hbm, time_hbm, down_hbm, gain_ref, z_ref,
    video_ref, space_ref, time_ref, down_ref,
    state, padded, ext, ext_in, cols, cols_in, corners, corners_in,
    late, late_in, u_hi, u_lo, a_hi, a_lo, d_hi, d_lo, w_space, w_time, w_hi, w_lo,
    send_sems, recv_sems, load_sems, greet, lowered_ready,
):
    tile = lax.axis_index("tile")
    frame = lax.axis_index("frame")
    loads = [
        pltpu.make_async_copy(video_hbm, video_ref, load_sems.at[0]),
        pltpu.make_async_copy(space_hbm, space_ref, load_sems.at[1]),
        pltpu.make_async_copy(time_hbm, time_ref, load_sems.at[2]),
        pltpu.make_async_copy(down_hbm, down_ref, load_sems.at[3]),
    ]
    for load in loads:
        load.start()
    k, z = tile // 4, tile % 4
    has_up, has_down = k > 0, k < 15
    has_left, has_right = z > 0, z < 3

    def dev(k, z, frame=frame):
        return {"tile": k * 4 + z, "frame": frame}

    def when(cond, fn):
        if cond is None:
            fn()
        else:
            pl.when(cond)(fn)

    ids = {}
    sent = []

    def message(name, src, dst, device):
        i = ids.setdefault(name, len(ids))
        return pltpu.make_async_remote_copy(
            src_ref=src, dst_ref=dst, send_sem=send_sems.at[i], recv_sem=recv_sems.at[i],
            device_id=device, device_id_type=MESH,
        )

    def start(name, src, dst, device, cond=None):
        copy = message(name, src, dst, device)
        when(cond, copy.start)
        sent.append((copy, cond))

    def arrived(name, ref, cond=None):
        copy = message(name, ref, ref, dev(k, (z + 1) % 4))
        when(cond, copy.wait_recv)

    for b in range(3):
        padded[b, :, :, 0:8, :] = jnp.zeros((4, 10, 8, 128), F32)
        padded[b, :, :, 48:56, :] = jnp.zeros((4, 10, 8, 128), F32)

        @pl.when(jnp.logical_not(has_up))
        def _():
            padded[b, :, 0, :, :] = jnp.zeros((4, 56, 128), F32)

        @pl.when(jnp.logical_not(has_down))
        def _():
            padded[b, :, 9, :, :] = jnp.zeros((4, 56, 128), F32)

    barrier = pltpu.get_barrier_semaphore()

    def hello(device, cond=None):
        when(cond, lambda: pl.semaphore_signal(barrier, inc=1, device_id=device, device_id_type=MESH))

    sides = ((-1, has_up), (1, has_down))
    flanks = ((-1, has_left), (1, has_right))
    for dz in range(1, 4):
        hello(dev(k, (z + dz) % 4))
    for dk, ok in sides:
        hello(dev((k + dk) % 16, z), ok)
        for dz, fine in flanks:
            hello(dev((k + dk) % 16, (z + dz) % 4), ok & fine)
    hello(dev(k, z, (frame + 3) % 4), frame > 0)
    count = 3 + (frame < 3).astype(jnp.int32)
    across = 1 + has_left.astype(jnp.int32) + has_right.astype(jnp.int32)
    count = count + (has_up.astype(jnp.int32) + has_down.astype(jnp.int32)) * across
    pl.semaphore_wait(barrier, count + greet(hello))

    order = (2, 3, 0, 1)

    def band(part):
        return pl.ds(pl.multiple_of(part * 40, 8), 40)

    for fr in order:
        for dz in (2, 1, 3):
            part = (z + dz) % 4
            start(("band", fr, dz), video_hbm.at[fr, :, band(part), :], state.at[fr, pl.ds(z * 2, 2)], dev(k, part))
    loads[0].wait()
    for part in range(4):
        for fr in range(4):
            if part == 0:
                ext[part, fr, 0:2] = jnp.zeros((2, 1, 128), F32)
            else:
                ext[part, fr, 0:2] = video_ref[fr, :, 40 * part - 1 : 40 * part, :]
            if part == 3:
                ext[part, fr, 2:4] = jnp.zeros((2, 1, 128), F32)
            else:
                ext[part, fr, 2:4] = video_ref[fr, :, 40 * part + 40 : 40 * part + 41, :]

    for dz in (2, 1, 3):
        part = (z + dz) % 4
        start(("ext", dz), ext.at[part], ext_in.at[z], dev(k, part))
    ext_in[z] = ext[z]
    for fr in range(4):
        state[fr, pl.ds(z * 2, 2)] = video_ref[fr, :, band(z), :]

    for load in loads[1:]:
        load.wait()
    for b in range(2):
        for tap in range(9):
            rows = slice(tap * 128, tap * 128 + 128)
            high, low = split(space_ref[b, rows, :])
            w_space[b, rows, 0:128] = high
            w_space[b, rows, 128:256] = low
        high, low = split(time_ref[b])
        w_time[b, :, 0:128] = high
        w_time[b, :, 128:256] = low
    for tap in range(9):
        rows = slice(tap * 128, tap * 128 + 128)
        high, low = split(down_ref[rows, :])
        w_hi[rows, :] = high
        w_lo[rows, :] = low

    def two_part(high, low, weight):
        both = jnp.dot(high, weight, preferred_element_type=F32)
        rest = jnp.dot(low, weight[:, 0:128], preferred_element_type=F32)
        return both[:, 0:128] + both[:, 128:256] + rest

    inner = pl.ds(8, 40)

    def send_rows(b, f0, nf, width, both=True):
        f = pl.ds(f0, nf)
        start(("row", b, f0, 1), padded.at[b, f, 8, width, :], padded.at[b, f, 0, width, :], dev((k + 1) % 16, z), has_down)
        if both:
            start(("row", b, f0, -1), padded.at[b, f, 1, width, :], padded.at[b, f, 9, width, :], dev((k + 15) % 16, z), has_up)

    def rows_arrived(b, f0, nf, width, both=True):
        f = pl.ds(f0, nf)
        arrived(("row", b, f0, 1), padded.at[b, f, 0, width, :], has_up)
        if both:
            arrived(("row", b, f0, -1), padded.at[b, f, 9, width, :], has_down)

    def directions(both):
        return ((1, 1), (1, -1), (-1, 1), (-1, -1)) if both else ((1, 1),)

    def send_edges(b, f0, nf, both=True):
        f = pl.ds(f0, nf)
        for fr in range(f0, f0 + nf):
            cols[b - 1, 1, fr] = padded[b, fr, 1:9, 47:48, :]
            if both:
                cols[b - 1, 0, fr] = padded[b, fr, 1:9, 8:9, :]
            for dk, dz in directions(both):
                row, col = 8 if dk > 0 else 1, 47 if dz > 0 else 8
                corners[b - 1, (dk > 0) * 2 + (dz > 0), fr] = padded[b, fr, row, col : col + 1, :]
        start(("col", b, f0, 1), cols.at[b - 1, 1, f], cols_in.at[b - 1, 1, f], dev(k, (z + 1) % 4), has_right)
        if both:
            start(("col", b, f0, -1), cols.at[b - 1, 0, f], cols_in.at[b - 1, 0, f], dev(k, (z + 3) % 4), has_left)
        for dk, dz in directions(both):
            c = (dk > 0) * 2 + (dz > 0)
            ok = (has_down if dk > 0 else has_up) & (has_right if dz > 0 else has_left)
            start(
                ("corner", b, f0, dk, dz), corners.at[b - 1, c, f], corners_in.at[b - 1, c, f],
                dev((k + dk) % 16, (z + dz) % 4), ok,
            )

    def edges_arrived(b, f0, nf, both=True):
        f = pl.ds(f0, nf)
        rows_arrived(b, f0, nf, inner, both)
        arrived(("col", b, f0, 1), cols_in.at[b - 1, 1, f], has_left)
        if both:
            arrived(("col", b, f0, -1), cols_in.at[b - 1, 0, f], has_right)

        @pl.when(has_left)
        def _():
            for fr in range(f0, f0 + nf):
                padded[b, fr, 1:9, LEFT : LEFT + 1, :] = cols_in[b - 1, 1, fr]

        if both:
            @pl.when(has_right)
            def _():
                for fr in range(f0, f0 + nf):
                    padded[b, fr, 1:9, RIGHT : RIGHT + 1, :] = cols_in[b - 1, 0, fr]

        for dk, dz in directions(both):
            c = (dk > 0) * 2 + (dz > 0)
            ok = (has_up if dk > 0 else has_down) & (has_left if dz > 0 else has_right)
            arrived(("corner", b, f0, dk, dz), corners_in.at[b - 1, c, f], ok)

            @pl.when(ok)
            def _():
                row, col = 0 if dk > 0 else 9, LEFT if dz > 0 else RIGHT
                for fr in range(f0, f0 + nf):
                    padded[b, fr, row, col : col + 1, :] = corners_in[b - 1, c, fr]

    def conv(b, fr):
        at = fr % 2
        for dx in range(3):
            window = padded[b, fr, :, LEFT + dx : LEFT + dx + 40, :]
            for dy in range(3):
                lanes = slice((dy * 3 + dx) * 128, (dy * 3 + dx) * 128 + 128)
                high, low = split(window[dy : dy + 8].reshape(320, 128))
                a_hi[at, :, lanes] = high
                a_lo[at, :, lanes] = low
        mixed = two_part(a_hi[at], a_lo[at], w_space[b])
        u = act(mixed, gain_ref[b, 1:2, :])
        put(fr, u)
        if fr >= 2:
            late[b, fr - 2] = u
            start(
                ("late", b, fr), late.at[b, fr - 2], late_in.at[b, fr - 2],
                dev(k, z, (frame + 1) % 4), frame < 3,
            )

    def put(fr, u):
        lanes = slice((fr + 2) * 128, (fr + 3) * 128)
        u_hi[:, lanes], u_lo[:, lanes] = split(u)

    def earlier(b):
        for fr in (2, 3):
            arrived(("late", b, fr), late_in.at[b, fr - 2], frame > 0)

        @pl.when(frame > 0)
        def _():
            put(-2, late_in[b, 0])
            put(-1, late_in[b, 1])

        @pl.when(frame == 0)
        def _():
            for parts in (u_hi, u_lo):
                parts[:, 0:128] = parts[:, 256:384]
                parts[:, 128:256] = parts[:, 256:384]

    def mix(b, fr):
        lanes = slice(fr * 128, fr * 128 + 384)
        return state[fr].reshape(320, 128) + two_part(u_hi[:, lanes], u_lo[:, lanes], w_time[b])

    for dz in range(1, 4):
        arrived(("ext", dz), ext_in.at[(z + dz) % 4])
    gain = gain_ref[0, 0:1, :]
    for at, fr in enumerate(order):
        for dz in range(1, 4):
            arrived(("band", fr, dz), state.at[fr, pl.ds(((z + dz) % 4) * 2, 2)])
        padded[0, fr, 1:9, 8:48, :] = act(state[fr].reshape(320, 128), gain).reshape(8, 40, 128)
        for src in range(4):
            fringe = act(ext_in[src, fr], gain)
            rows = slice(1 + 2 * src, 3 + 2 * src)

            @pl.when(has_left)
            def _():
                padded[0, fr, rows, LEFT : LEFT + 1, :] = fringe[0:2]

            @pl.when(has_right)
            def _():
                padded[0, fr, rows, RIGHT : RIGHT + 1, :] = fringe[2:4]
        send_rows(0, fr, 1, slice(None))
        if at > 0:
            rows_arrived(0, order[at - 1], 1, slice(None))
            conv(0, order[at - 1])
    rows_arrived(0, order[3], 1, slice(None))
    conv(0, order[3])

    gain = gain_ref[1, 0:1, :]

    def middle(f0):
        for fr in (f0, f0 + 1):
            x = mix(0, fr)
            padded[1, fr, 1:9, 8:48, :] = act(x, gain).reshape(8, 40, 128)
            state[fr] = x.reshape(8, 40, 128)
        send_rows(1, f0, 2, inner)
        send_edges(1, f0, 2)

    middle(2)
    edges_arrived(1, 2, 2)
    for fr in (2, 3):
        conv(1, fr)
    earlier(0)
    middle(0)
    edges_arrived(1, 0, 2)
    for fr in (0, 1):
        conv(1, fr)
    for f0 in (2, 0):
        if f0 == 0:
            earlier(1)
        for fr in (f0, f0 + 1):
            padded[2, fr, 1:9, 8:48, :] = mix(1, fr).reshape(8, 40, 128)
        send_rows(2, f0, 2, inner, False)
        send_edges(2, f0, 2, False)

    for f0 in (2, 0):
        edges_arrived(2, f0, 2, False)
        for fr in (f0, f0 + 1):
            for row in range(4):
                at = slice((fr - f0) * 96 + row * 24, (fr - f0) * 96 + row * 24 + 24)
                for dy in range(3):
                    for dx in range(3):
                        taken = padded[2, fr, 2 * row + dy, pl.ds(LEFT + dx, 24, stride=2), :]
                        lanes = slice((dy * 3 + dx) * 128, (dy * 3 + dx) * 128 + 128)
                        high = taken.astype(BF16).astype(F32)
                        d_hi[at, lanes] = high
                        d_lo[at, lanes] = taken - high
        high, low = d_hi[...].astype(BF16), d_lo[...].astype(BF16)
        lowered = jnp.dot(high, w_hi[...], preferred_element_type=F32)
        lowered = lowered + jnp.dot(high, w_lo[...], preferred_element_type=F32)
        lowered = lowered + jnp.dot(low, w_hi[...], preferred_element_type=F32)
        for fr in (f0, f0 + 1):
            for row in range(4):
                for part in range(4):
                    at = (fr - f0) * 96 + row * 24 + part * 5
                    z_ref[fr, part * 20 + row * 5 : part * 20 + row * 5 + 5, :] = lowered[at : at + 5]
            lowered_ready(fr)

    def finish():
        for copy, cond in sent:
            when(cond, copy.wait_send)

    return finish


def dot_f32(a, b, dims=((1,), (0,))):
    return lax.dot_general(a, b, (dims, ((), ())), precision=highest, preferred_element_type=F32)


def attend_part(
    gain_ref, loads, wq_ref, wk_ref, wv_ref, wo_ref, z_ref, out_ref,
    keys, q_hi, q_lo, q_own, q_in, acc, best, total, part_acc, part_stat, result, landing, k_hi_ref, k_lo_ref,
    s1, r1, ss, rs, rets, retr,
):
    tile = lax.axis_index("tile")
    frame = lax.axis_index("frame")
    x, y, z = tile // 16, (tile // 4) % 4, tile % 4
    half, s = z // 2, z % 2
    zh, core = frame // 2, frame % 2

    def dev(x, y, z, core):
        return {"tile": x * 16 + y * 4 + z, "frame": zh * 2 + core}

    up = dev(x, (y + 1) % 4, z, core)
    down = dev(x, (y + 3) % 4, z, core)
    mate = dev(x, y, z + 1 - 2 * s, core)
    sibling = dev(x, y, z, 1 - core)
    sz = 2 * core + s
    crossed = half != core
    uncrossed = jnp.logical_not(crossed)

    from_z, from_core = 2 * core + y % 2, y // 2

    def greet(hello):
        for device in (up, down, mate, sibling):
            hello(device)
        for dx in range(1, 4):
            hello(dev((x + dx) % 4, y, sz, half))
        hello(dev(x, y, sz, half), crossed)
        expected = 7 + crossed.astype(jnp.int32)
        for j in range(4):
            hello(
                dev(x, j, from_z, from_core),
                jnp.logical_not((j == y) & (from_z == z) & (from_core == core)),
            )
            expected = expected + jnp.logical_not((sz == y) & (z == j) & (half == core)).astype(jnp.int32)
        return expected

    slot = s * 4 + y

    def block(b):
        return pl.ds(b * 80, 80)

    mine = pl.ds(pl.multiple_of(x * 80, 80), 80)

    def to_group(fr):
        return pltpu.make_async_remote_copy(
            src_ref=z_ref.at[fr],
            dst_ref=keys.at[slot, mine],
            send_sem=s1.at[fr],
            recv_sem=r1.at[x],
            device_id=dev(fr, y, sz, half),
            device_id_type=MESH,
        )

    def lowered_ready(fr):
        stays = uncrossed & (x == fr)

        @pl.when(jnp.logical_not(stays))
        def _():
            to_group(fr).start()

        @pl.when(stays)
        def _():
            keys[slot, mine, :] = z_ref[fr]

    def run():
        sent = []
        slot_up = s * 4 + (y + 1) % 4
        slot_down = s * 4 + (y + 3) % 4
        slot_far = s * 4 + (y + 2) % 4
        other = (1 - s) * 4
        mate_own, mate_up = other + y, other + (y + 1) % 4
        mate_down, mate_far = other + (y + 3) % 4, other + (y + 2) % 4

        def remote(src, dst, device, i):
            return pltpu.make_async_remote_copy(
                src_ref=src, dst_ref=dst, send_sem=ss.at[i], recv_sem=rs.at[i],
                device_id=device, device_id_type=MESH,
            )

        own_up, own_down, own_mate, mate_goes_up, mate_goes_down, far_on, far_mate = range(7)

        def push(kind, b, source, device):
            ref = keys.at[source, block(b)]
            copy = remote(ref, ref, device, kind * 4 + b)
            copy.start()
            sent.append(copy)

        def landed(kind, b, source):
            ref = keys.at[source, block(b)]
            remote(ref, ref, sibling, kind * 4 + b).wait_recv()

        for b in range(4):
            @pl.when(jnp.logical_not(uncrossed & (x == b)))
            def _():
                pltpu.make_async_remote_copy(
                    src_ref=z_ref.at[0],
                    dst_ref=keys.at[slot, block(b)],
                    send_sem=s1.at[b],
                    recv_sem=r1.at[b],
                    device_id=sibling,
                    device_id_type=MESH,
                ).wait_recv()

            push(own_up, b, slot, up)
            push(own_down, b, slot, down)
            push(own_mate, b, slot, mate)
        for load in loads:
            load.wait()

        gain = gain_ref[...]
        projected = dot_f32(norm(keys[slot], gain), wq_ref[...]) * (256.0 ** -0.5)
        q_own[...] = dot_f32(projected, wk_ref[...], ((1,), (1,)))
        q_copy = remote(q_own, q_in, sibling, 28)
        q_copy.start()
        sent.append(q_copy)
        q_hi[0:320], q_lo[0:320] = split(q_own[...])

        best[...] = jnp.full_like(best, -jnp.inf)
        total[...] = jnp.zeros_like(total)
        acc[...] = jnp.zeros_like(acc)

        def product(a, b, dims):
            return lax.dot_general(a, b, (dims, ((), ())), preferred_element_type=F32)

        def prepare(at, source):
            place = slice(at * 320, at * 320 + 320)
            k_hi_ref[place], k_lo_ref[place] = split(norm(keys[source], gain))

        def attend(start, stop, rows):
            k_hi, k_lo = k_hi_ref[start * 320 : stop * 320], k_lo_ref[start * 320 : stop * 320]
            across = ((1,), (1,))
            scores = product(q_hi[rows], k_hi, across) + product(q_hi[rows], k_lo, across)
            scores = scores + product(q_lo[rows], k_hi, across)
            old = best[rows]
            new = jnp.maximum(old, jnp.max(scores, axis=1, keepdims=True))
            factor = jnp.exp(old - new)
            weights = jnp.exp(scores - new)
            total[rows] = total[rows] * factor + jnp.sum(weights, axis=1, keepdims=True)
            best[rows] = new
            p_hi, p_lo = split(weights)
            along = ((1,), (0,))
            mixed = product(p_hi, k_hi, along) + product(p_hi, k_lo, along) + product(p_lo, k_hi, along)
            acc[rows] = acc[rows] * factor + mixed

        first, second, both = slice(0, 320), slice(320, 640), slice(0, 640)

        def forward(b):
            if b < 2:
                landed(own_up, b, slot_down)
                push(far_on, b, slot_down, up)
                landed(own_down, b, slot_up)
            else:
                landed(own_down, b, slot_up)
                push(far_on, b, slot_up, down)
                landed(own_up, b, slot_down)
            landed(own_mate, b, mate_own)
            push(mate_goes_up, b, mate_own, up)
            push(mate_goes_down, b, mate_own, down)

        def far_forward(b):
            landed(far_on, b, slot_far)
            push(far_mate, b, slot_far, mate)

        forward(0)
        prepare(0, slot)
        attend(0, 1, first)
        forward(1)
        q_copy.wait_recv()
        q_hi[320:640], q_lo[320:640] = split(q_in[...])
        attend(0, 1, second)
        forward(2)
        forward(3)
        prepare(1, slot_down)
        far_forward(0)
        prepare(2, slot_up)
        far_forward(1)
        far_forward(2)
        prepare(3, mate_own)
        far_forward(3)
        prepare(4, slot_far)
        attend(1, 5, both)
        for b in range(4):
            landed(mate_goes_up, b, mate_down)
        prepare(5, mate_down)
        for b in range(4):
            landed(mate_goes_down, b, mate_up)
        prepare(6, mate_up)
        for b in range(4):
            landed(far_mate, b, mate_far)
        prepare(7, mate_far)
        attend(5, 8, second)
        part_stat[0, :, 0:64] = jnp.broadcast_to(best[second], (320, 64))
        part_stat[0, :, 64:128] = jnp.broadcast_to(total[second], (320, 64))
        merge = [
            remote(part_stat.at[0], part_stat.at[1], sibling, 30),
            remote(acc.at[pl.ds(320, 320)], part_acc, sibling, 29),
        ]
        for copy in merge:
            copy.start()
        attend(5, 8, first)
        for copy in merge:
            copy.wait_recv()
        sent.extend(merge)
        other_best = part_stat[1, :, 0:1]
        other_total = part_stat[1, :, 64:65]
        top = jnp.maximum(best[first], other_best)
        mine_f = jnp.exp(best[first] - top)
        other_f = jnp.exp(other_best - top)
        whole = total[first] * mine_f + other_total * other_f
        mixed = (acc[first] * mine_f + part_acc[...] * other_f) / whole
        value = dot_f32(mixed, wv_ref[...])
        y_out = keys[slot] + dot_f32(value, wo_ref[...])

        backs = []
        for part in range(4):
            for b in range(4):
                start = b * 80 + part * 20
                result[part, b] = y_out[start : start + 20]
            copy = pltpu.make_async_remote_copy(
                src_ref=result.at[part],
                dst_ref=landing.at[:, y],
                send_sem=rets.at[part],
                recv_sem=retr.at[y],
                device_id=dev(x, sz, part, half),
                device_id_type=MESH,
            )
            stays = (sz == y) & (z == part) & (half == core)
            backs.append((copy, stays))

            @pl.when(jnp.logical_not(stays))
            def _():
                copy.start()

            @pl.when(stays)
            def _():
                landing[:, pl.ds(y, 1), :, :] = result[part][:, None]

        for sy in range(4):
            here = (sy == y) & (from_z == z) & (from_core == core)

            @pl.when(jnp.logical_not(here))
            def _():
                pltpu.make_async_remote_copy(
                    src_ref=result.at[0],
                    dst_ref=landing.at[:, sy],
                    send_sem=rets.at[0],
                    recv_sem=retr.at[sy],
                    device_id=sibling,
                    device_id_type=MESH,
                ).wait_recv()

            for sx in range(4):
                at = (sx * 4 + sy) * 20
                out_ref[0, at : at + 20, :] = landing[sx, sy]

        for fr in range(4):
            @pl.when(jnp.logical_not(uncrossed & (x == fr)))
            def _():
                to_group(fr).wait_send()

        for copy in sent:
            copy.wait_send()
        for copy, stays in backs:
            @pl.when(jnp.logical_not(stays))
            def _():
                copy.wait_send()

    return greet, lowered_ready, run


CONV_SCRATCH = [
    ((4, 2, 160, 128), F32), ((2, 1152, 128), F32), ((2, 384, 128), F32), ((1152, 256), F32),
    ((4, 8, 40, 128), F32), ((3, 4, 10, 56, 128), F32), ((4, 4, 4, 1, 128), F32), ((4, 4, 4, 1, 128), F32),
    ((2, 2, 4, 8, 1, 128), F32), ((2, 2, 4, 8, 1, 128), F32), ((2, 4, 4, 1, 128), F32), ((2, 4, 4, 1, 128), F32),
    ((2, 2, 320, 128), F32), ((2, 2, 320, 128), F32), ((320, 768), BF16), ((320, 768), BF16),
    ((2, 320, 1152), BF16), ((2, 320, 1152), BF16), ((192, 1152), F32), ((192, 1152), F32),
    ((2, 1152, 256), BF16), ((2, 384, 256), BF16), ((1152, 256), BF16), ((1152, 256), BF16),
]
ATTEND_SCRATCH = [
    ((8, 320, 256), F32), ((640, 256), BF16), ((640, 256), BF16), ((320, 256), F32), ((320, 256), F32),
    ((640, 256), F32), ((640, 1), F32), ((640, 1), F32), ((320, 256), F32), ((2, 320, 128), F32),
    ((4, 4, 20, 256), F32), ((4, 4, 20, 256), F32), ((2560, 256), BF16), ((2560, 256), BF16),
]
CONV_SEMS = (56, 56)
ATTEND_SEMS = (4, 4, 31, 31, 4, 4)


def encode_kernel(
    video_hbm, space_hbm, time_hbm, down_hbm, wq_hbm, wk_hbm, wv_hbm, wo_hbm, gain_ref, attn_gain_ref, out_ref,
    z_ref, wq_ref, wk_ref, wv_ref, wo_ref, load_sems, *scratch,
):
    c, a = len(CONV_SCRATCH), len(ATTEND_SCRATCH)
    conv_scratch, attend_scratch = scratch[:c], scratch[c : c + a]
    conv_sems, attend_sems = scratch[c + a : c + a + 2], scratch[c + a + 2 :]
    pairs = ((wq_hbm, wq_ref), (wk_hbm, wk_ref), (wv_hbm, wv_ref), (wo_hbm, wo_ref))
    loads = [pltpu.make_async_copy(src, dst, load_sems.at[4 + i]) for i, (src, dst) in enumerate(pairs)]
    greet, lowered_ready, attend = attend_part(
        attn_gain_ref, loads, wq_ref, wk_ref, wv_ref, wo_ref, z_ref, out_ref, *attend_scratch, *attend_sems
    )
    for load in loads:
        load.start()
    finish = conv_part(
        video_hbm, space_hbm, time_hbm, down_hbm, gain_ref, z_ref, *conv_scratch, *conv_sems,
        load_sems, greet, lowered_ready,
    )
    attend()
    finish()


def local(
    video,
    norm_gain,
    space_weight,
    time_weight,
    down_weight,
    attn_gain,
    w_query,
    w_key,
    w_value,
    w_out,
):
    vmem = pl.BlockSpec(memory_space=pltpu.VMEM)
    hbm = pl.BlockSpec(memory_space=pltpu.HBM)
    dma = pltpu.SemaphoreType.DMA
    square = pltpu.VMEM((256, 256), F32)
    return pl.pallas_call(
        encode_kernel,
        out_shape=jax.ShapeDtypeStruct((1, 320, 256), F32),
        in_specs=[hbm] * 8 + [vmem] * 2,
        out_specs=vmem,
        scratch_shapes=[
            pltpu.VMEM((4, 80, 256), F32), square, square, square, square, dma((8,)),
            *[pltpu.VMEM(shape, dtype) for shape, dtype in CONV_SCRATCH + ATTEND_SCRATCH],
            *[dma((count,)) for count in CONV_SEMS + ATTEND_SEMS],
        ],
        compiler_params=pltpu.CompilerParams(
            collective_id=3, has_side_effects=True, vmem_limit_bytes=56 * 2**20
        ),
        name="encode",
    )(
        video, space_weight.reshape(2, 1152, 128), time_weight.reshape(2, 384, 128), down_weight.reshape(1152, 256),
        w_query, w_key, w_value, w_out, norm_gain, attn_gain.reshape(1, 256),
    )


def solution(mesh):
    in_specs = (P("frame", "tile", None, None), P(), P(), P(), P(), P(), P(), P(), P(), P())
    out_specs = P(("frame", "tile"), None, None)
    return jax.shard_map(local, mesh=mesh, in_specs=in_specs, out_specs=out_specs, check_vma=False)
```

```python
import jax
import jax.numpy as jnp
from jax import lax
from jax.experimental import pallas as pl
from jax.experimental.pallas import tpu as pltpu
from jax.sharding import PartitionSpec as P

highest = lax.Precision.HIGHEST
MESH = pl.DeviceIdType.MESH
F32 = jnp.float32
BF16 = jnp.bfloat16


def norm(values, gain):
    return values * lax.rsqrt(jnp.mean(values * values, -1, keepdims=True) + 1e-06) * gain


def split(values):
    high = values.astype(BF16)
    return high, (values - high.astype(F32)).astype(BF16)


LEFT, RIGHT = 7, 48


def act(values, gain):
    scaled = values * lax.rsqrt(jnp.mean(values * values, -1, keepdims=True) + 1e-06) * gain
    return scaled / (1.0 + jnp.exp(-scaled))


def conv_part(
    video_hbm, space_hbm, time_hbm, down_hbm, gain_ref, z_ref,
    video_ref, space_ref, time_ref, down_ref,
    state, padded, ext, ext_in, cols, cols_in, corners, corners_in,
    late, late_in, u_hi, u_lo, a_hi, a_lo, d_hi, d_lo, w_space, w_time, w_hi, w_lo,
    send_sems, recv_sems, load_sems, greet, weights_ready, lowered_ready,
):
    tile = lax.axis_index("tile")
    frame = lax.axis_index("frame")
    loads = [
        pltpu.make_async_copy(video_hbm, video_ref, load_sems.at[0]),
        pltpu.make_async_copy(space_hbm, space_ref, load_sems.at[1]),
        pltpu.make_async_copy(time_hbm, time_ref, load_sems.at[2]),
        pltpu.make_async_copy(down_hbm, down_ref, load_sems.at[3]),
    ]
    for load in loads:
        load.start()
    k, z = tile // 4, tile % 4
    has_up, has_down = k > 0, k < 15
    has_left, has_right = z > 0, z < 3

    def dev(k, z, frame=frame):
        return {"tile": k * 4 + z, "frame": frame}

    def when(cond, fn):
        if cond is None:
            fn()
        else:
            pl.when(cond)(fn)

    ids = {}
    sent = []

    def message(name, src, dst, device):
        i = ids.setdefault(name, len(ids))
        return pltpu.make_async_remote_copy(
            src_ref=src, dst_ref=dst, send_sem=send_sems.at[i], recv_sem=recv_sems.at[i],
            device_id=device, device_id_type=MESH,
        )

    def start(name, src, dst, device, cond=None):
        copy = message(name, src, dst, device)
        when(cond, copy.start)
        sent.append((copy, cond))

    def arrived(name, ref, cond=None):
        copy = message(name, ref, ref, dev(k, (z + 1) % 4))
        when(cond, copy.wait_recv)

    for b in range(3):
        padded[b, :, :, 0:8, :] = jnp.zeros((4, 10, 8, 128), F32)
        padded[b, :, :, 48:56, :] = jnp.zeros((4, 10, 8, 128), F32)

        @pl.when(jnp.logical_not(has_up))
        def _():
            padded[b, :, 0, :, :] = jnp.zeros((4, 56, 128), F32)

        @pl.when(jnp.logical_not(has_down))
        def _():
            padded[b, :, 9, :, :] = jnp.zeros((4, 56, 128), F32)

    barrier = pltpu.get_barrier_semaphore()

    def hello(device, cond=None):
        when(cond, lambda: pl.semaphore_signal(barrier, inc=1, device_id=device, device_id_type=MESH))

    sides = ((-1, has_up), (1, has_down))
    flanks = ((-1, has_left), (1, has_right))
    for dz in range(1, 4):
        hello(dev(k, (z + dz) % 4))
    for dk, ok in sides:
        hello(dev((k + dk) % 16, z), ok)
        for dz, fine in flanks:
            hello(dev((k + dk) % 16, (z + dz) % 4), ok & fine)
    hello(dev(k, z, (frame + 3) % 4), frame > 0)
    count = 3 + (frame < 3).astype(jnp.int32)
    across = 1 + has_left.astype(jnp.int32) + has_right.astype(jnp.int32)
    count = count + (has_up.astype(jnp.int32) + has_down.astype(jnp.int32)) * across
    pl.semaphore_wait(barrier, count + greet(hello))

    order = (2, 3, 0, 1)

    def band(part):
        return pl.ds(pl.multiple_of(part * 40, 8), 40)

    for fr in order:
        for dz in (2, 1, 3):
            part = (z + dz) % 4
            start(("band", fr, dz), video_hbm.at[fr, :, band(part), :], state.at[fr, pl.ds(z * 2, 2)], dev(k, part))
    loads[0].wait()
    for part in range(4):
        for fr in range(4):
            if part == 0:
                ext[part, fr, 0:2] = jnp.zeros((2, 1, 128), F32)
            else:
                ext[part, fr, 0:2] = video_ref[fr, :, 40 * part - 1 : 40 * part, :]
            if part == 3:
                ext[part, fr, 2:4] = jnp.zeros((2, 1, 128), F32)
            else:
                ext[part, fr, 2:4] = video_ref[fr, :, 40 * part + 40 : 40 * part + 41, :]

    for dz in (2, 1, 3):
        part = (z + dz) % 4
        start(("ext", dz), ext.at[part], ext_in.at[z], dev(k, part))
    ext_in[z] = ext[z]
    for fr in range(4):
        state[fr, pl.ds(z * 2, 2)] = video_ref[fr, :, band(z), :]

    for load in loads[1:]:
        load.wait()
    for b in range(2):
        for tap in range(9):
            rows = slice(tap * 128, tap * 128 + 128)
            high, low = split(space_ref[b, rows, :])
            w_space[b, rows, 0:128] = high
            w_space[b, rows, 128:256] = low
        high, low = split(time_ref[b])
        w_time[b, :, 0:128] = high
        w_time[b, :, 128:256] = low
    for tap in range(9):
        rows = slice(tap * 128, tap * 128 + 128)
        high, low = split(down_ref[rows, :])
        w_hi[rows, :] = high
        w_lo[rows, :] = low
    weights_ready()

    def two_part(high, low, weight):
        both = jnp.dot(high, weight, preferred_element_type=F32)
        rest = jnp.dot(low, weight[:, 0:128], preferred_element_type=F32)
        return both[:, 0:128] + both[:, 128:256] + rest

    inner = pl.ds(8, 40)

    def send_rows(b, f0, nf, width, both=True):
        f = pl.ds(f0, nf)
        start(("row", b, f0, 1), padded.at[b, f, 8, width, :], padded.at[b, f, 0, width, :], dev((k + 1) % 16, z), has_down)
        if both:
            start(("row", b, f0, -1), padded.at[b, f, 1, width, :], padded.at[b, f, 9, width, :], dev((k + 15) % 16, z), has_up)

    def rows_arrived(b, f0, nf, width, both=True):
        f = pl.ds(f0, nf)
        arrived(("row", b, f0, 1), padded.at[b, f, 0, width, :], has_up)
        if both:
            arrived(("row", b, f0, -1), padded.at[b, f, 9, width, :], has_down)

    def directions(both):
        return ((1, 1), (1, -1), (-1, 1), (-1, -1)) if both else ((1, 1),)

    def send_edges(b, f0, nf, both=True):
        f = pl.ds(f0, nf)
        for fr in range(f0, f0 + nf):
            cols[b - 1, 1, fr] = padded[b, fr, 1:9, 47:48, :]
            if both:
                cols[b - 1, 0, fr] = padded[b, fr, 1:9, 8:9, :]
            for dk, dz in directions(both):
                row, col = 8 if dk > 0 else 1, 47 if dz > 0 else 8
                corners[b - 1, (dk > 0) * 2 + (dz > 0), fr] = padded[b, fr, row, col : col + 1, :]
        start(("col", b, f0, 1), cols.at[b - 1, 1, f], cols_in.at[b - 1, 1, f], dev(k, (z + 1) % 4), has_right)
        if both:
            start(("col", b, f0, -1), cols.at[b - 1, 0, f], cols_in.at[b - 1, 0, f], dev(k, (z + 3) % 4), has_left)
        for dk, dz in directions(both):
            c = (dk > 0) * 2 + (dz > 0)
            ok = (has_down if dk > 0 else has_up) & (has_right if dz > 0 else has_left)
            start(
                ("corner", b, f0, dk, dz), corners.at[b - 1, c, f], corners_in.at[b - 1, c, f],
                dev((k + dk) % 16, (z + dz) % 4), ok,
            )

    def edges_arrived(b, f0, nf, both=True):
        f = pl.ds(f0, nf)
        rows_arrived(b, f0, nf, inner, both)
        arrived(("col", b, f0, 1), cols_in.at[b - 1, 1, f], has_left)
        if both:
            arrived(("col", b, f0, -1), cols_in.at[b - 1, 0, f], has_right)

        @pl.when(has_left)
        def _():
            for fr in range(f0, f0 + nf):
                padded[b, fr, 1:9, LEFT : LEFT + 1, :] = cols_in[b - 1, 1, fr]

        if both:
            @pl.when(has_right)
            def _():
                for fr in range(f0, f0 + nf):
                    padded[b, fr, 1:9, RIGHT : RIGHT + 1, :] = cols_in[b - 1, 0, fr]

        for dk, dz in directions(both):
            c = (dk > 0) * 2 + (dz > 0)
            ok = (has_up if dk > 0 else has_down) & (has_left if dz > 0 else has_right)
            arrived(("corner", b, f0, dk, dz), corners_in.at[b - 1, c, f], ok)

            @pl.when(ok)
            def _():
                row, col = 0 if dk > 0 else 9, LEFT if dz > 0 else RIGHT
                for fr in range(f0, f0 + nf):
                    padded[b, fr, row, col : col + 1, :] = corners_in[b - 1, c, fr]

    def conv(b, fr):
        at = fr % 2
        for dx in range(3):
            window = padded[b, fr, :, LEFT + dx : LEFT + dx + 40, :]
            for dy in range(3):
                lanes = slice((dy * 3 + dx) * 128, (dy * 3 + dx) * 128 + 128)
                high, low = split(window[dy : dy + 8].reshape(320, 128))
                a_hi[at, :, lanes] = high
                a_lo[at, :, lanes] = low
        mixed = two_part(a_hi[at], a_lo[at], w_space[b])
        u = act(mixed, gain_ref[b, 1:2, :])
        put(fr, u)
        if fr >= 2:
            late[b, fr - 2] = u
            start(
                ("late", b, fr), late.at[b, fr - 2], late_in.at[b, fr - 2],
                dev(k, z, (frame + 1) % 4), frame < 3,
            )

    def put(fr, u):
        lanes = slice((fr + 2) * 128, (fr + 3) * 128)
        u_hi[:, lanes], u_lo[:, lanes] = split(u)

    def earlier(b):
        for fr in (2, 3):
            arrived(("late", b, fr), late_in.at[b, fr - 2], frame > 0)

        @pl.when(frame > 0)
        def _():
            put(-2, late_in[b, 0])
            put(-1, late_in[b, 1])

        @pl.when(frame == 0)
        def _():
            for parts in (u_hi, u_lo):
                parts[:, 0:128] = parts[:, 256:384]
                parts[:, 128:256] = parts[:, 256:384]

    def mix(b, fr):
        lanes = slice(fr * 128, fr * 128 + 384)
        return state[fr].reshape(320, 128) + two_part(u_hi[:, lanes], u_lo[:, lanes], w_time[b])

    for dz in range(1, 4):
        arrived(("ext", dz), ext_in.at[(z + dz) % 4])
    gain = gain_ref[0, 0:1, :]
    for fr in order:
        for dz in range(1, 4):
            arrived(("band", fr, dz), state.at[fr, pl.ds(((z + dz) % 4) * 2, 2)])
        padded[0, fr, 1:9, 8:48, :] = act(state[fr].reshape(320, 128), gain).reshape(8, 40, 128)
        for src in range(4):
            fringe = act(ext_in[src, fr], gain)
            rows = slice(1 + 2 * src, 3 + 2 * src)

            @pl.when(has_left)
            def _():
                padded[0, fr, rows, LEFT : LEFT + 1, :] = fringe[0:2]

            @pl.when(has_right)
            def _():
                padded[0, fr, rows, RIGHT : RIGHT + 1, :] = fringe[2:4]
        send_rows(0, fr, 1, slice(None))
    for fr in order:
        rows_arrived(0, fr, 1, slice(None))
        conv(0, fr)

    gain = gain_ref[1, 0:1, :]

    def middle(f0):
        for fr in (f0, f0 + 1):
            x = mix(0, fr)
            padded[1, fr, 1:9, 8:48, :] = act(x, gain).reshape(8, 40, 128)
            state[fr] = x.reshape(8, 40, 128)
        send_rows(1, f0, 2, inner)
        send_edges(1, f0, 2)

    middle(2)
    earlier(0)
    middle(0)
    for f0 in (2, 0):
        edges_arrived(1, f0, 2)
        for fr in (f0, f0 + 1):
            conv(1, fr)
    for f0 in (2, 0):
        if f0 == 0:
            earlier(1)
        for fr in (f0, f0 + 1):
            padded[2, fr, 1:9, 8:48, :] = mix(1, fr).reshape(8, 40, 128)
        send_rows(2, f0, 2, inner, False)
        send_edges(2, f0, 2, False)

    def take(f0, row, dy, dx):
        lanes = slice((dy * 3 + dx) * 128, (dy * 3 + dx) * 128 + 128)
        for fr in (f0, f0 + 1):
            at = slice((fr - f0) * 96 + row * 24, (fr - f0) * 96 + row * 24 + 24)
            taken = padded[2, fr, 2 * row + dy, pl.ds(LEFT + dx, 24, stride=2), :]
            high = taken.astype(BF16).astype(F32)
            d_hi[at, lanes] = high
            d_lo[at, lanes] = taken - high

    taps = [(row, dy, dx) for row in range(4) for dy in range(3) for dx in range(3)]
    for f0 in (2, 0):
        for row, dy, dx in taps:
            if dx > 0 and row + dy > 0:
                take(f0, row, dy, dx)
        edges_arrived(2, f0, 2, False)
        for row, dy, dx in taps:
            if dx == 0 or row + dy == 0:
                take(f0, row, dy, dx)
        high, low = d_hi[...].astype(BF16), d_lo[...].astype(BF16)
        lowered = jnp.dot(high, w_hi[...], preferred_element_type=F32)
        lowered = lowered + jnp.dot(high, w_lo[...], preferred_element_type=F32)
        lowered = lowered + jnp.dot(low, w_hi[...], preferred_element_type=F32)
        for fr in (f0, f0 + 1):
            for row in range(4):
                for part in range(4):
                    at = (fr - f0) * 96 + row * 24 + part * 5
                    z_ref[fr, part * 20 + row * 5 : part * 20 + row * 5 + 5, :] = lowered[at : at + 5]
            lowered_ready(fr)

    def finish():
        for copy, cond in sent:
            when(cond, copy.wait_send)

    return finish


def dot_f32(a, b, dims=((1,), (0,))):
    return lax.dot_general(a, b, (dims, ((), ())), precision=highest, preferred_element_type=F32)


def attend_part(
    gain_ref, loads, wq_ref, wk_ref, wv_ref, wo_ref, z_ref, out_ref,
    keys, q_ref, q_own, q_in, acc, best, total, part_acc, part_stat, result, landing, k_ref, own_z, w_qk, w_vo,
    s1, r1, ss, rs, rets, retr,
):
    tile = lax.axis_index("tile")
    frame = lax.axis_index("frame")
    x, y, z = tile // 16, (tile // 4) % 4, tile % 4
    half, s = z // 2, z % 2
    zh, core = frame // 2, frame % 2

    def dev(x, y, z, core):
        return {"tile": x * 16 + y * 4 + z, "frame": zh * 2 + core}

    up = dev(x, (y + 1) % 4, z, core)
    down = dev(x, (y + 3) % 4, z, core)
    mate = dev(x, y, z + 1 - 2 * s, core)
    sibling = dev(x, y, z, 1 - core)
    sz = 2 * core + s
    crossed = half != core
    uncrossed = jnp.logical_not(crossed)

    from_z, from_core = 2 * core + y % 2, y // 2

    def greet(hello):
        for device in (up, down, mate, sibling):
            hello(device)
        for dx in range(1, 4):
            hello(dev((x + dx) % 4, y, sz, half))
        hello(dev(x, y, sz, half), crossed)
        expected = 7 + crossed.astype(jnp.int32)
        for j in range(4):
            hello(
                dev(x, j, from_z, from_core),
                jnp.logical_not((j == y) & (from_z == z) & (from_core == core)),
            )
            expected = expected + jnp.logical_not((sz == y) & (z == j) & (half == core)).astype(jnp.int32)
        return expected

    slot = s * 4 + y

    def block(b):
        return pl.ds(b * 80, 80)

    mine = pl.ds(pl.multiple_of(x * 80, 80), 80)

    def to_group(fr):
        return pltpu.make_async_remote_copy(
            src_ref=z_ref.at[fr],
            dst_ref=own_z.at[mine],
            send_sem=s1.at[fr],
            recv_sem=r1.at[x],
            device_id=dev(fr, y, sz, half),
            device_id_type=MESH,
        )

    def lowered_ready(fr):
        stays = uncrossed & (x == fr)

        @pl.when(jnp.logical_not(stays))
        def _():
            to_group(fr).start()

        @pl.when(stays)
        def _():
            own_z[mine, :] = z_ref[fr]

    def weights_ready():
        for load in loads:
            load.wait()
        together = dot_f32(wq_ref[...], wk_ref[...], ((1,), (1,))) * (256.0 ** -0.5 * 1.4426950408889634)
        w_qk[0], w_qk[1] = split(together)
        w_vo[0], w_vo[1] = split(dot_f32(wv_ref[...], wo_ref[...]))

    def three_part(values, weight):
        high, low = split(values)
        total = jnp.dot(high, weight[0], preferred_element_type=F32)
        total = total + jnp.dot(high, weight[1], preferred_element_type=F32)
        return total + jnp.dot(low, weight[0], preferred_element_type=F32)

    def run():
        sent = []
        slot_up = s * 4 + (y + 1) % 4
        slot_down = s * 4 + (y + 3) % 4
        slot_far = s * 4 + (y + 2) % 4
        other = (1 - s) * 4
        mate_own, mate_up = other + y, other + (y + 1) % 4
        mate_down, mate_far = other + (y + 3) % 4, other + (y + 2) % 4

        def remote(src, dst, device, i):
            return pltpu.make_async_remote_copy(
                src_ref=src, dst_ref=dst, send_sem=ss.at[i], recv_sem=rs.at[i],
                device_id=device, device_id_type=MESH,
            )

        own_up, own_down, own_mate, mate_goes_up, mate_goes_down, far_on, far_mate = range(7)

        def push(kind, b, source, device):
            ref = keys.at[source, block(b)]
            copy = remote(ref, ref, device, kind * 4 + b)
            copy.start()
            sent.append(copy)

        def landed(kind, b, source):
            ref = keys.at[source, block(b)]
            remote(ref, ref, sibling, kind * 4 + b).wait_recv()

        gain = gain_ref[...]
        for b in range(4):
            @pl.when(jnp.logical_not(uncrossed & (x == b)))
            def _():
                pltpu.make_async_remote_copy(
                    src_ref=z_ref.at[0],
                    dst_ref=own_z.at[block(b)],
                    send_sem=s1.at[b],
                    recv_sem=r1.at[b],
                    device_id=sibling,
                    device_id_type=MESH,
                ).wait_recv()

            keys[slot, block(b), :] = norm(own_z[block(b)], gain)
            push(own_up, b, slot, up)
            push(own_down, b, slot, down)
            push(own_mate, b, slot, mate)
        def place_query(at, values):
            rows = slice(at, at + 320)
            high, low = split(values[...])
            q_ref[rows, 0:256] = high
            q_ref[rows, 256:512] = low
            q_ref[rows, 512:768] = high

        q_own[...] = three_part(keys[slot], w_qk)
        q_copy = remote(q_own, q_in, sibling, 28)
        q_copy.start()
        sent.append(q_copy)
        place_query(0, q_own)

        best[...] = jnp.full_like(best, -jnp.inf)
        total[...] = jnp.zeros_like(total)
        acc[...] = jnp.zeros_like(acc)

        def product(a, b, dims):
            return lax.dot_general(a, b, (dims, ((), ())), preferred_element_type=F32)

        def prepare(at, source):
            place = slice(at * 320, at * 320 + 320)
            high, low = split(keys[source])
            k_ref[place, 0:256] = high
            k_ref[place, 256:512] = high
            k_ref[place, 512:768] = low

        def attend(start, stop, rows):
            place = slice(start * 320, stop * 320)
            k_hi, k_lo = k_ref[place, 0:256], k_ref[place, 512:768]
            scores = product(q_ref[rows], k_ref[place], ((1,), (1,)))
            old = best[rows]
            new = jnp.maximum(old, jnp.max(scores, axis=1, keepdims=True))
            factor = jnp.exp2(old - new)
            weights = jnp.exp2(scores - new)
            total[rows] = total[rows] * factor + jnp.sum(weights, axis=1, keepdims=True)
            best[rows] = new
            p_hi, p_lo = split(weights)
            along = ((1,), (0,))
            mixed = product(p_hi, k_hi, along) + product(p_hi, k_lo, along) + product(p_lo, k_hi, along)
            acc[rows] = acc[rows] * factor + mixed

        first, second = slice(0, 320), slice(320, 640)

        def forward(b):
            if b < 2:
                landed(own_up, b, slot_down)
                push(far_on, b, slot_down, up)
                landed(own_down, b, slot_up)
            else:
                landed(own_down, b, slot_up)
                push(far_on, b, slot_up, down)
                landed(own_up, b, slot_down)
            landed(own_mate, b, mate_own)
            push(mate_goes_up, b, mate_own, up)
            push(mate_goes_down, b, mate_own, down)

        def far_forward(b):
            landed(far_on, b, slot_far)
            push(far_mate, b, slot_far, mate)

        forward(0)
        prepare(0, slot)
        attend(0, 1, first)
        forward(1)
        q_copy.wait_recv()
        place_query(320, q_in)
        attend(0, 1, second)
        forward(2)
        forward(3)
        prepare(1, slot_down)
        far_forward(0)
        prepare(2, slot_up)
        far_forward(1)
        far_forward(2)
        prepare(3, mate_own)
        far_forward(3)
        prepare(4, slot_far)
        attend(1, 5, second)
        attend(1, 5, first)
        for b in range(4):
            landed(mate_goes_up, b, mate_down)
        prepare(5, mate_down)
        for b in range(4):
            landed(mate_goes_down, b, mate_up)
        prepare(6, mate_up)
        for b in range(4):
            landed(far_mate, b, mate_far)
        prepare(7, mate_far)
        attend(5, 8, second)
        part_stat[0, :, 0:64] = jnp.broadcast_to(best[second], (320, 64))
        part_stat[0, :, 64:128] = jnp.broadcast_to(total[second], (320, 64))
        merge = [
            remote(part_stat.at[0], part_stat.at[1], sibling, 30),
            remote(acc.at[pl.ds(320, 320)], part_acc, sibling, 29),
        ]
        for copy in merge:
            copy.start()
        attend(5, 8, first)
        for copy in merge:
            copy.wait_recv()
        sent.extend(merge)
        other_best = part_stat[1, :, 0:1]
        other_total = part_stat[1, :, 64:65]
        top = jnp.maximum(best[first], other_best)
        mine_f = jnp.exp2(best[first] - top)
        other_f = jnp.exp2(other_best - top)
        whole = total[first] * mine_f + other_total * other_f
        mixed = (acc[first] * mine_f + part_acc[...] * other_f) / whole
        y_out = own_z[...] + three_part(mixed, w_vo)

        backs = []
        for part in range(4):
            for b in range(4):
                start = b * 80 + part * 20
                result[part, b * 20 : b * 20 + 20] = y_out[start : start + 20]
            copy = pltpu.make_async_remote_copy(
                src_ref=result.at[part],
                dst_ref=landing.at[y],
                send_sem=rets.at[part],
                recv_sem=retr.at[y],
                device_id=dev(x, sz, part, half),
                device_id_type=MESH,
            )
            stays = (sz == y) & (z == part) & (half == core)
            backs.append((copy, stays))

            @pl.when(jnp.logical_not(stays))
            def _():
                copy.start()

            @pl.when(stays)
            def _():
                landing[y] = result[part]

        for sy in range(4):
            here = (sy == y) & (from_z == z) & (from_core == core)

            @pl.when(jnp.logical_not(here))
            def _():
                pltpu.make_async_remote_copy(
                    src_ref=result.at[0],
                    dst_ref=landing.at[sy],
                    send_sem=rets.at[0],
                    recv_sem=retr.at[sy],
                    device_id=sibling,
                    device_id_type=MESH,
                ).wait_recv()

            for sx in range(4):
                at = (sx * 4 + sy) * 20
                out_ref[0, at : at + 20, :] = landing[sy, sx * 20 : sx * 20 + 20]

        for fr in range(4):
            @pl.when(jnp.logical_not(uncrossed & (x == fr)))
            def _():
                to_group(fr).wait_send()

        for copy in sent:
            copy.wait_send()
        for copy, stays in backs:
            @pl.when(jnp.logical_not(stays))
            def _():
                copy.wait_send()

    return greet, weights_ready, lowered_ready, run


CONV_SCRATCH = [
    ((4, 2, 160, 128), F32), ((2, 1152, 128), F32), ((2, 384, 128), F32), ((1152, 256), F32),
    ((4, 8, 40, 128), F32), ((3, 4, 10, 56, 128), F32), ((4, 4, 4, 1, 128), F32), ((4, 4, 4, 1, 128), F32),
    ((2, 2, 4, 8, 1, 128), F32), ((2, 2, 4, 8, 1, 128), F32), ((2, 4, 4, 1, 128), F32), ((2, 4, 4, 1, 128), F32),
    ((2, 2, 320, 128), F32), ((2, 2, 320, 128), F32), ((320, 768), BF16), ((320, 768), BF16),
    ((2, 320, 1152), BF16), ((2, 320, 1152), BF16), ((192, 1152), F32), ((192, 1152), F32),
    ((2, 1152, 256), BF16), ((2, 384, 256), BF16), ((1152, 256), BF16), ((1152, 256), BF16),
]
ATTEND_SCRATCH = [
    ((8, 320, 256), F32), ((640, 768), BF16), ((320, 256), F32), ((320, 256), F32),
    ((640, 256), F32), ((640, 1), F32), ((640, 1), F32), ((320, 256), F32), ((2, 320, 128), F32),
    ((4, 80, 256), F32), ((4, 80, 256), F32), ((2560, 768), BF16),
    ((320, 256), F32), ((2, 256, 256), BF16), ((2, 256, 256), BF16),
]
CONV_SEMS = (56, 56)
ATTEND_SEMS = (4, 4, 31, 31, 4, 4)


def encode_kernel(
    video_hbm, space_hbm, time_hbm, down_hbm, wq_hbm, wk_hbm, wv_hbm, wo_hbm, gain_ref, attn_gain_ref, out_ref,
    z_ref, wq_ref, wk_ref, wv_ref, wo_ref, load_sems, *scratch,
):
    c, a = len(CONV_SCRATCH), len(ATTEND_SCRATCH)
    conv_scratch, attend_scratch = scratch[:c], scratch[c : c + a]
    conv_sems, attend_sems = scratch[c + a : c + a + 2], scratch[c + a + 2 :]
    pairs = ((wq_hbm, wq_ref), (wk_hbm, wk_ref), (wv_hbm, wv_ref), (wo_hbm, wo_ref))
    loads = [pltpu.make_async_copy(src, dst, load_sems.at[4 + i]) for i, (src, dst) in enumerate(pairs)]
    greet, weights_ready, lowered_ready, attend = attend_part(
        attn_gain_ref, loads, wq_ref, wk_ref, wv_ref, wo_ref, z_ref, out_ref, *attend_scratch, *attend_sems
    )
    for load in loads:
        load.start()
    finish = conv_part(
        video_hbm, space_hbm, time_hbm, down_hbm, gain_ref, z_ref, *conv_scratch, *conv_sems,
        load_sems, greet, weights_ready, lowered_ready,
    )
    attend()
    finish()


def local(
    video,
    norm_gain,
    space_weight,
    time_weight,
    down_weight,
    attn_gain,
    w_query,
    w_key,
    w_value,
    w_out,
):
    vmem = pl.BlockSpec(memory_space=pltpu.VMEM)
    hbm = pl.BlockSpec(memory_space=pltpu.HBM)
    dma = pltpu.SemaphoreType.DMA
    square = pltpu.VMEM((256, 256), F32)
    return pl.pallas_call(
        encode_kernel,
        out_shape=jax.ShapeDtypeStruct((1, 320, 256), F32),
        in_specs=[hbm] * 8 + [vmem] * 2,
        out_specs=vmem,
        scratch_shapes=[
            pltpu.VMEM((4, 80, 256), F32), square, square, square, square, dma((8,)),
            *[pltpu.VMEM(shape, dtype) for shape, dtype in CONV_SCRATCH + ATTEND_SCRATCH],
            *[dma((count,)) for count in CONV_SEMS + ATTEND_SEMS],
        ],
        compiler_params=pltpu.CompilerParams(
            collective_id=3, has_side_effects=True, vmem_limit_bytes=56 * 2**20
        ),
        name="encode",
    )(
        video, space_weight.reshape(2, 1152, 128), time_weight.reshape(2, 384, 128), down_weight.reshape(1152, 256),
        w_query, w_key, w_value, w_out, norm_gain, attn_gain.reshape(1, 256),
    )


def solution(mesh):
    in_specs = (P("frame", "tile", None, None), P(), P(), P(), P(), P(), P(), P(), P(), P())
    out_specs = P(("frame", "tile"), None, None)
    return jax.shard_map(local, mesh=mesh, in_specs=in_specs, out_specs=out_specs, check_vma=False)
```

```python
import jax
import jax.numpy as jnp
from jax import lax
from jax.experimental import pallas as pl
from jax.experimental.pallas import tpu as pltpu
from jax.sharding import PartitionSpec as P

highest = lax.Precision.HIGHEST
MESH = pl.DeviceIdType.MESH
F32 = jnp.float32
BF16 = jnp.bfloat16


def norm(values, gain):
    return values * lax.rsqrt(jnp.mean(values * values, -1, keepdims=True) + 1e-06) * gain


def split(values):
    high = values.astype(BF16)
    return high, (values - high.astype(F32)).astype(BF16)


LEFT, RIGHT = 7, 48


def act(values, gain):
    scaled = values * lax.rsqrt(jnp.mean(values * values, -1, keepdims=True) + 1e-06) * gain
    return scaled / (1.0 + jnp.exp(-scaled))


def conv_part(
    video_hbm, space_hbm, time_hbm, down_hbm, gain_ref, z_ref,
    video_ref, space_ref, time_ref, down_ref,
    state, padded, ext, ext_in, cols, cols_in, corners, corners_in,
    late, late_in, u_hi, u_lo, a_hi, a_lo, d_hi, d_lo, w_space, w_time, w_hi, w_lo,
    send_sems, recv_sems, load_sems, greet, weights_ready, lowered_ready,
):
    tile = lax.axis_index("tile")
    frame = lax.axis_index("frame")
    loads = [
        pltpu.make_async_copy(video_hbm, video_ref, load_sems.at[0]),
        pltpu.make_async_copy(space_hbm, space_ref, load_sems.at[1]),
        pltpu.make_async_copy(time_hbm, time_ref, load_sems.at[2]),
        pltpu.make_async_copy(down_hbm, down_ref, load_sems.at[3]),
    ]
    for load in loads:
        load.start()
    k, z = tile // 4, tile % 4
    has_up, has_down = k > 0, k < 15
    has_left, has_right = z > 0, z < 3

    def dev(k, z, frame=frame):
        return {"tile": k * 4 + z, "frame": frame}

    def when(cond, fn):
        if cond is None:
            fn()
        else:
            pl.when(cond)(fn)

    ids = {}
    sent = []

    def message(name, src, dst, device):
        i = ids.setdefault(name, len(ids))
        return pltpu.make_async_remote_copy(
            src_ref=src, dst_ref=dst, send_sem=send_sems.at[i], recv_sem=recv_sems.at[i],
            device_id=device, device_id_type=MESH,
        )

    def start(name, src, dst, device, cond=None):
        copy = message(name, src, dst, device)
        when(cond, copy.start)
        sent.append((copy, cond))

    def arrived(name, ref, cond=None):
        copy = message(name, ref, ref, dev(k, (z + 1) % 4))
        when(cond, copy.wait_recv)

    for b in range(3):
        padded[b, :, :, 0:8, :] = jnp.zeros((4, 10, 8, 128), F32)
        padded[b, :, :, 48:56, :] = jnp.zeros((4, 10, 8, 128), F32)

        @pl.when(jnp.logical_not(has_up))
        def _():
            padded[b, :, 0, :, :] = jnp.zeros((4, 56, 128), F32)

        @pl.when(jnp.logical_not(has_down))
        def _():
            padded[b, :, 9, :, :] = jnp.zeros((4, 56, 128), F32)

    barrier = pltpu.get_barrier_semaphore()

    def hello(device, cond=None):
        when(cond, lambda: pl.semaphore_signal(barrier, inc=1, device_id=device, device_id_type=MESH))

    sides = ((-1, has_up), (1, has_down))
    flanks = ((-1, has_left), (1, has_right))
    for dz in range(1, 4):
        hello(dev(k, (z + dz) % 4))
    for dk, ok in sides:
        hello(dev((k + dk) % 16, z), ok)
        for dz, fine in flanks:
            hello(dev((k + dk) % 16, (z + dz) % 4), ok & fine)
    hello(dev(k, z, (frame + 3) % 4), frame > 0)
    count = 3 + (frame < 3).astype(jnp.int32)
    across = 1 + has_left.astype(jnp.int32) + has_right.astype(jnp.int32)
    count = count + (has_up.astype(jnp.int32) + has_down.astype(jnp.int32)) * across
    pl.semaphore_wait(barrier, count + greet(hello))

    order = (2, 3, 0, 1)

    def band(part):
        return pl.ds(pl.multiple_of(part * 40, 8), 40)

    def send_bands(fr):
        for dz in (2, 1, 3):
            part = (z + dz) % 4
            start(("band", fr, dz), video_hbm.at[fr, :, band(part), :], state.at[fr, pl.ds(z * 2, 2)], dev(k, part))

    def bands_left():
        for copy, _ in sent[:3]:
            copy.wait_send()
        sent[:3] = []

    send_bands(2)
    send_bands(3)
    loads[0].wait()
    for part in range(4):
        for fr in range(4):
            if part == 0:
                ext[part, fr, 0:2] = jnp.zeros((2, 1, 128), F32)
            else:
                ext[part, fr, 0:2] = video_ref[fr, :, 40 * part - 1 : 40 * part, :]
            if part == 3:
                ext[part, fr, 2:4] = jnp.zeros((2, 1, 128), F32)
            else:
                ext[part, fr, 2:4] = video_ref[fr, :, 40 * part + 40 : 40 * part + 41, :]

    for dz in (2, 1, 3):
        part = (z + dz) % 4
        start(("ext", dz), ext.at[part], ext_in.at[z], dev(k, part))
    ext_in[z] = ext[z]
    for fr in range(4):
        state[fr, pl.ds(z * 2, 2)] = video_ref[fr, :, band(z), :]

    for load in loads[1:]:
        load.wait()
    for b in range(2):
        for tap in range(9):
            rows = slice(tap * 128, tap * 128 + 128)
            high, low = split(space_ref[b, rows, :])
            w_space[b, rows, 0:128] = high
            w_space[b, rows, 128:256] = low
        high, low = split(time_ref[b])
        w_time[b, :, 0:128] = high
        w_time[b, :, 128:256] = low
    for tap in range(9):
        rows = slice(tap * 128, tap * 128 + 128)
        high, low = split(down_ref[rows, :])
        w_hi[rows, :] = high
        w_lo[rows, :] = low
    weights_ready()

    def two_part(high, low, weight):
        both = jnp.dot(high, weight, preferred_element_type=F32)
        rest = jnp.dot(low, weight[:, 0:128], preferred_element_type=F32)
        return both[:, 0:128] + both[:, 128:256] + rest

    inner = pl.ds(8, 40)

    def send_rows(b, f0, nf, width, both=True):
        f = pl.ds(f0, nf)
        start(("row", b, f0, 1), padded.at[b, f, 8, width, :], padded.at[b, f, 0, width, :], dev((k + 1) % 16, z), has_down)
        if both:
            start(("row", b, f0, -1), padded.at[b, f, 1, width, :], padded.at[b, f, 9, width, :], dev((k + 15) % 16, z), has_up)

    def rows_arrived(b, f0, nf, width, both=True):
        f = pl.ds(f0, nf)
        arrived(("row", b, f0, 1), padded.at[b, f, 0, width, :], has_up)
        if both:
            arrived(("row", b, f0, -1), padded.at[b, f, 9, width, :], has_down)

    def directions(both):
        return ((1, 1), (1, -1), (-1, 1), (-1, -1)) if both else ((1, 1),)

    def send_edges(b, f0, nf, both=True):
        f = pl.ds(f0, nf)
        for fr in range(f0, f0 + nf):
            cols[b - 1, 1, fr] = padded[b, fr, 1:9, 47:48, :]
            if both:
                cols[b - 1, 0, fr] = padded[b, fr, 1:9, 8:9, :]
            for dk, dz in directions(both):
                row, col = 8 if dk > 0 else 1, 47 if dz > 0 else 8
                corners[b - 1, (dk > 0) * 2 + (dz > 0), fr] = padded[b, fr, row, col : col + 1, :]
        start(("col", b, f0, 1), cols.at[b - 1, 1, f], cols_in.at[b - 1, 1, f], dev(k, (z + 1) % 4), has_right)
        if both:
            start(("col", b, f0, -1), cols.at[b - 1, 0, f], cols_in.at[b - 1, 0, f], dev(k, (z + 3) % 4), has_left)
        for dk, dz in directions(both):
            c = (dk > 0) * 2 + (dz > 0)
            ok = (has_down if dk > 0 else has_up) & (has_right if dz > 0 else has_left)
            start(
                ("corner", b, f0, dk, dz), corners.at[b - 1, c, f], corners_in.at[b - 1, c, f],
                dev((k + dk) % 16, (z + dz) % 4), ok,
            )

    def edges_arrived(b, f0, nf, both=True):
        f = pl.ds(f0, nf)
        rows_arrived(b, f0, nf, inner, both)
        arrived(("col", b, f0, 1), cols_in.at[b - 1, 1, f], has_left)
        if both:
            arrived(("col", b, f0, -1), cols_in.at[b - 1, 0, f], has_right)

        @pl.when(has_left)
        def _():
            for fr in range(f0, f0 + nf):
                padded[b, fr, 1:9, LEFT : LEFT + 1, :] = cols_in[b - 1, 1, fr]

        if both:
            @pl.when(has_right)
            def _():
                for fr in range(f0, f0 + nf):
                    padded[b, fr, 1:9, RIGHT : RIGHT + 1, :] = cols_in[b - 1, 0, fr]

        for dk, dz in directions(both):
            c = (dk > 0) * 2 + (dz > 0)
            ok = (has_up if dk > 0 else has_down) & (has_left if dz > 0 else has_right)
            arrived(("corner", b, f0, dk, dz), corners_in.at[b - 1, c, f], ok)

            @pl.when(ok)
            def _():
                row, col = 0 if dk > 0 else 9, LEFT if dz > 0 else RIGHT
                for fr in range(f0, f0 + nf):
                    padded[b, fr, row, col : col + 1, :] = corners_in[b - 1, c, fr]

    def conv(b, fr):
        at = fr % 2
        for dx in range(3):
            window = padded[b, fr, :, LEFT + dx : LEFT + dx + 40, :]
            for dy in range(3):
                lanes = slice((dy * 3 + dx) * 128, (dy * 3 + dx) * 128 + 128)
                high, low = split(window[dy : dy + 8].reshape(320, 128))
                a_hi[at, :, lanes] = high
                a_lo[at, :, lanes] = low
        mixed = two_part(a_hi[at], a_lo[at], w_space[b])
        u = act(mixed, gain_ref[b, 1:2, :])
        put(fr, u)
        if fr >= 2:
            late[b, fr - 2] = u
            start(
                ("late", b, fr), late.at[b, fr - 2], late_in.at[b, fr - 2],
                dev(k, z, (frame + 1) % 4), frame < 3,
            )

    def put(fr, u):
        lanes = slice((fr + 2) * 128, (fr + 3) * 128)
        u_hi[:, lanes], u_lo[:, lanes] = split(u)

    def earlier(b):
        for fr in (2, 3):
            arrived(("late", b, fr), late_in.at[b, fr - 2], frame > 0)

        @pl.when(frame > 0)
        def _():
            put(-2, late_in[b, 0])
            put(-1, late_in[b, 1])

        @pl.when(frame == 0)
        def _():
            for parts in (u_hi, u_lo):
                parts[:, 0:128] = parts[:, 256:384]
                parts[:, 128:256] = parts[:, 256:384]

    def mix(b, fr):
        lanes = slice(fr * 128, fr * 128 + 384)
        return state[fr].reshape(320, 128) + two_part(u_hi[:, lanes], u_lo[:, lanes], w_time[b])

    bands_left()
    send_bands(0)

    for dz in range(1, 4):
        arrived(("ext", dz), ext_in.at[(z + dz) % 4])
    gain = gain_ref[0, 0:1, :]
    for fr in order:
        if fr == 3:
            bands_left()
            send_bands(1)
        for dz in range(1, 4):
            arrived(("band", fr, dz), state.at[fr, pl.ds(((z + dz) % 4) * 2, 2)])
        padded[0, fr, 1:9, 8:48, :] = act(state[fr].reshape(320, 128), gain).reshape(8, 40, 128)
        for src in range(4):
            fringe = act(ext_in[src, fr], gain)
            rows = slice(1 + 2 * src, 3 + 2 * src)

            @pl.when(has_left)
            def _():
                padded[0, fr, rows, LEFT : LEFT + 1, :] = fringe[0:2]

            @pl.when(has_right)
            def _():
                padded[0, fr, rows, RIGHT : RIGHT + 1, :] = fringe[2:4]
        send_rows(0, fr, 1, slice(None))
        if fr < 2:
            rows_arrived(0, fr + 2, 1, slice(None))
            conv(0, fr + 2)
    for fr in (0, 1):
        rows_arrived(0, fr, 1, slice(None))
        conv(0, fr)

    gain = gain_ref[1, 0:1, :]

    def middle(f0):
        for fr in (f0, f0 + 1):
            x = mix(0, fr)
            padded[1, fr, 1:9, 8:48, :] = act(x, gain).reshape(8, 40, 128)
            state[fr] = x.reshape(8, 40, 128)
        send_rows(1, f0, 2, inner)
        send_edges(1, f0, 2)

    middle(2)
    earlier(0)
    middle(0)
    for f0 in (2, 0):
        edges_arrived(1, f0, 2)
        for fr in (f0, f0 + 1):
            conv(1, fr)
    for f0 in (2, 0):
        if f0 == 0:
            earlier(1)
        for fr in (f0, f0 + 1):
            padded[2, fr, 1:9, 8:48, :] = mix(1, fr).reshape(8, 40, 128)
        send_rows(2, f0, 2, inner, False)
        send_edges(2, f0, 2, False)

    def take(f0, row, dy, dx):
        lanes = slice((dy * 3 + dx) * 128, (dy * 3 + dx) * 128 + 128)
        for fr in (f0, f0 + 1):
            at = slice((fr - f0) * 96 + row * 24, (fr - f0) * 96 + row * 24 + 24)
            taken = padded[2, fr, 2 * row + dy, pl.ds(LEFT + dx, 24, stride=2), :]
            high = taken.astype(BF16).astype(F32)
            d_hi[at, lanes] = high
            d_lo[at, lanes] = taken - high

    taps = [(row, dy, dx) for row in range(4) for dy in range(3) for dx in range(3)]
    for f0 in (2, 0):
        for row, dy, dx in taps:
            if dx > 0 and row + dy > 0:
                take(f0, row, dy, dx)
        edges_arrived(2, f0, 2, False)
        for row, dy, dx in taps:
            if dx == 0 or row + dy == 0:
                take(f0, row, dy, dx)
        high, low = d_hi[...].astype(BF16), d_lo[...].astype(BF16)
        lowered = jnp.dot(high, w_hi[...], preferred_element_type=F32)
        lowered = lowered + jnp.dot(high, w_lo[...], preferred_element_type=F32)
        lowered = lowered + jnp.dot(low, w_hi[...], preferred_element_type=F32)
        for fr in (f0, f0 + 1):
            for row in range(4):
                for part in range(4):
                    at = (fr - f0) * 96 + row * 24 + part * 5
                    z_ref[fr, part * 20 + row * 5 : part * 20 + row * 5 + 5, :] = lowered[at : at + 5]
            lowered_ready(fr)

    def finish():
        for copy, cond in sent:
            when(cond, copy.wait_send)

    return finish


def dot_f32(a, b, dims=((1,), (0,))):
    return lax.dot_general(a, b, (dims, ((), ())), precision=highest, preferred_element_type=F32)


def attend_part(
    gain_ref, loads, wq_ref, wk_ref, wv_ref, wo_ref, z_ref, out_ref,
    keys, q_ref, q_own, q_in, acc, best, total, part_acc, part_stat, result, landing, k_ref, own_z, w_qk, w_vo,
    s1, r1, ss, rs, rets, retr,
):
    tile = lax.axis_index("tile")
    frame = lax.axis_index("frame")
    x, y, z = tile // 16, (tile // 4) % 4, tile % 4
    half, s = z // 2, z % 2
    zh, core = frame // 2, frame % 2

    def dev(x, y, z, core):
        return {"tile": x * 16 + y * 4 + z, "frame": zh * 2 + core}

    up = dev(x, (y + 1) % 4, z, core)
    down = dev(x, (y + 3) % 4, z, core)
    mate = dev(x, y, z + 1 - 2 * s, core)
    sibling = dev(x, y, z, 1 - core)
    sz = 2 * core + s
    crossed = half != core
    uncrossed = jnp.logical_not(crossed)

    from_z, from_core = 2 * core + y % 2, y // 2

    def greet(hello):
        for device in (up, down, mate, sibling):
            hello(device)
        for dx in range(1, 4):
            hello(dev((x + dx) % 4, y, sz, half))
        hello(dev(x, y, sz, half), crossed)
        expected = 7 + crossed.astype(jnp.int32)
        for j in range(4):
            hello(
                dev(x, j, from_z, from_core),
                jnp.logical_not((j == y) & (from_z == z) & (from_core == core)),
            )
            expected = expected + jnp.logical_not((sz == y) & (z == j) & (half == core)).astype(jnp.int32)
        return expected

    slot = s * 4 + y

    def block(b):
        return pl.ds(b * 80, 80)

    mine = pl.ds(pl.multiple_of(x * 80, 80), 80)

    def to_group(fr):
        return pltpu.make_async_remote_copy(
            src_ref=z_ref.at[fr],
            dst_ref=own_z.at[mine],
            send_sem=s1.at[fr],
            recv_sem=r1.at[x],
            device_id=dev(fr, y, sz, half),
            device_id_type=MESH,
        )

    def lowered_ready(fr):
        stays = uncrossed & (x == fr)

        @pl.when(jnp.logical_not(stays))
        def _():
            to_group(fr).start()

        @pl.when(stays)
        def _():
            own_z[mine, :] = z_ref[fr]

    def weights_ready():
        for load in loads:
            load.wait()
        together = dot_f32(wq_ref[...], wk_ref[...], ((1,), (1,))) * (256.0 ** -0.5 * 1.4426950408889634)
        w_qk[0], w_qk[1] = split(together)
        w_vo[0], w_vo[1] = split(dot_f32(wv_ref[...], wo_ref[...]))

    def three_part(values, weight):
        high, low = split(values)
        total = jnp.dot(high, weight[0], preferred_element_type=F32)
        total = total + jnp.dot(high, weight[1], preferred_element_type=F32)
        return total + jnp.dot(low, weight[0], preferred_element_type=F32)

    def run():
        sent = []
        slot_up = s * 4 + (y + 1) % 4
        slot_down = s * 4 + (y + 3) % 4
        slot_far = s * 4 + (y + 2) % 4
        other = (1 - s) * 4
        mate_own, mate_up = other + y, other + (y + 1) % 4
        mate_down, mate_far = other + (y + 3) % 4, other + (y + 2) % 4

        def remote(src, dst, device, i):
            return pltpu.make_async_remote_copy(
                src_ref=src, dst_ref=dst, send_sem=ss.at[i], recv_sem=rs.at[i],
                device_id=device, device_id_type=MESH,
            )

        own_up, own_down, own_mate, mate_goes_up, mate_goes_down, far_on, far_mate = range(7)

        def push(kind, b, source, device):
            ref = keys.at[source, block(b)]
            copy = remote(ref, ref, device, kind * 4 + b)
            copy.start()
            sent.append(copy)

        def landed(kind, b, source):
            ref = keys.at[source, block(b)]
            remote(ref, ref, sibling, kind * 4 + b).wait_recv()

        gain = gain_ref[...]
        for b in range(4):
            @pl.when(jnp.logical_not(uncrossed & (x == b)))
            def _():
                pltpu.make_async_remote_copy(
                    src_ref=z_ref.at[0],
                    dst_ref=own_z.at[block(b)],
                    send_sem=s1.at[b],
                    recv_sem=r1.at[b],
                    device_id=sibling,
                    device_id_type=MESH,
                ).wait_recv()

            keys[slot, block(b), :] = norm(own_z[block(b)], gain)
            push(own_up, b, slot, up)
            push(own_down, b, slot, down)
            push(own_mate, b, slot, mate)
        def place_query(at, values):
            rows = slice(at, at + 320)
            high, low = split(values[...])
            q_ref[rows, 0:256] = high
            q_ref[rows, 256:512] = low
            q_ref[rows, 512:768] = high

        q_own[...] = three_part(keys[slot], w_qk)
        q_copy = remote(q_own, q_in, sibling, 28)
        q_copy.start()
        sent.append(q_copy)
        place_query(0, q_own)

        best[...] = jnp.full_like(best, -jnp.inf)
        total[...] = jnp.zeros_like(total)
        acc[...] = jnp.zeros_like(acc)

        def product(a, b, dims):
            return lax.dot_general(a, b, (dims, ((), ())), preferred_element_type=F32)

        def prepare(at, source):
            place = slice(at * 320, at * 320 + 320)
            high, low = split(keys[source])
            k_ref[place, 0:256] = high
            k_ref[place, 256:512] = high
            k_ref[place, 512:768] = low

        def attend(start, stop, rows):
            place = slice(start * 320, stop * 320)
            k_hi, k_lo = k_ref[place, 0:256], k_ref[place, 512:768]
            scores = product(q_ref[rows], k_ref[place], ((1,), (1,)))
            old = best[rows]
            new = jnp.maximum(old, jnp.max(scores, axis=1, keepdims=True))
            factor = jnp.exp2(old - new)
            weights = jnp.exp2(scores - new)
            total[rows] = total[rows] * factor + jnp.sum(weights, axis=1, keepdims=True)
            best[rows] = new
            p_hi, p_lo = split(weights)
            along = ((1,), (0,))
            mixed = product(p_hi, k_hi, along) + product(p_hi, k_lo, along) + product(p_lo, k_hi, along)
            acc[rows] = acc[rows] * factor + mixed

        first, second = slice(0, 320), slice(320, 640)

        def forward(b):
            if b < 2:
                landed(own_up, b, slot_down)
                push(far_on, b, slot_down, up)
                landed(own_down, b, slot_up)
            else:
                landed(own_down, b, slot_up)
                push(far_on, b, slot_up, down)
                landed(own_up, b, slot_down)
            landed(own_mate, b, mate_own)
            push(mate_goes_up, b, mate_own, up)
            push(mate_goes_down, b, mate_own, down)

        def far_forward(b):
            landed(far_on, b, slot_far)
            push(far_mate, b, slot_far, mate)

        forward(0)
        prepare(0, slot)
        attend(0, 1, first)
        forward(1)
        q_copy.wait_recv()
        place_query(320, q_in)
        attend(0, 1, second)
        forward(2)
        forward(3)
        prepare(1, slot_down)
        far_forward(0)
        prepare(2, slot_up)
        far_forward(1)
        far_forward(2)
        prepare(3, mate_own)
        far_forward(3)
        prepare(4, slot_far)
        attend(1, 5, second)
        attend(1, 5, first)
        for b in range(4):
            landed(mate_goes_up, b, mate_down)
        prepare(5, mate_down)
        for b in range(4):
            landed(mate_goes_down, b, mate_up)
        prepare(6, mate_up)
        for b in range(4):
            landed(far_mate, b, mate_far)
        prepare(7, mate_far)
        attend(5, 8, second)
        part_stat[0, :, 0:64] = jnp.broadcast_to(best[second], (320, 64))
        part_stat[0, :, 64:128] = jnp.broadcast_to(total[second], (320, 64))
        merge = [
            remote(part_stat.at[0], part_stat.at[1], sibling, 30),
            remote(acc.at[pl.ds(320, 320)], part_acc, sibling, 29),
        ]
        for copy in merge:
            copy.start()
        attend(5, 8, first)
        for copy in merge:
            copy.wait_recv()
        sent.extend(merge)
        other_best = part_stat[1, :, 0:1]
        other_total = part_stat[1, :, 64:65]
        top = jnp.maximum(best[first], other_best)
        mine_f = jnp.exp2(best[first] - top)
        other_f = jnp.exp2(other_best - top)
        whole = total[first] * mine_f + other_total * other_f
        mixed = (acc[first] * mine_f + part_acc[...] * other_f) / whole
        y_out = own_z[...] + three_part(mixed, w_vo)

        backs = []
        for part in range(4):
            for b in range(4):
                start = b * 80 + part * 20
                result[part, b * 20 : b * 20 + 20] = y_out[start : start + 20]
            copy = pltpu.make_async_remote_copy(
                src_ref=result.at[part],
                dst_ref=landing.at[y],
                send_sem=rets.at[part],
                recv_sem=retr.at[y],
                device_id=dev(x, sz, part, half),
                device_id_type=MESH,
            )
            stays = (sz == y) & (z == part) & (half == core)
            backs.append((copy, stays))

            @pl.when(jnp.logical_not(stays))
            def _():
                copy.start()

            @pl.when(stays)
            def _():
                landing[y] = result[part]

        for sy in range(4):
            here = (sy == y) & (from_z == z) & (from_core == core)

            @pl.when(jnp.logical_not(here))
            def _():
                pltpu.make_async_remote_copy(
                    src_ref=result.at[0],
                    dst_ref=landing.at[sy],
                    send_sem=rets.at[0],
                    recv_sem=retr.at[sy],
                    device_id=sibling,
                    device_id_type=MESH,
                ).wait_recv()

            for sx in range(4):
                at = (sx * 4 + sy) * 20
                out_ref[0, at : at + 20, :] = landing[sy, sx * 20 : sx * 20 + 20]

        for fr in range(4):
            @pl.when(jnp.logical_not(uncrossed & (x == fr)))
            def _():
                to_group(fr).wait_send()

        for copy in sent:
            copy.wait_send()
        for copy, stays in backs:
            @pl.when(jnp.logical_not(stays))
            def _():
                copy.wait_send()

    return greet, weights_ready, lowered_ready, run


CONV_SCRATCH = [
    ((4, 2, 160, 128), F32), ((2, 1152, 128), F32), ((2, 384, 128), F32), ((1152, 256), F32),
    ((4, 8, 40, 128), F32), ((3, 4, 10, 56, 128), F32), ((4, 4, 4, 1, 128), F32), ((4, 4, 4, 1, 128), F32),
    ((2, 2, 4, 8, 1, 128), F32), ((2, 2, 4, 8, 1, 128), F32), ((2, 4, 4, 1, 128), F32), ((2, 4, 4, 1, 128), F32),
    ((2, 2, 320, 128), F32), ((2, 2, 320, 128), F32), ((320, 768), BF16), ((320, 768), BF16),
    ((2, 320, 1152), BF16), ((2, 320, 1152), BF16), ((192, 1152), F32), ((192, 1152), F32),
    ((2, 1152, 256), BF16), ((2, 384, 256), BF16), ((1152, 256), BF16), ((1152, 256), BF16),
]
ATTEND_SCRATCH = [
    ((8, 320, 256), F32), ((640, 768), BF16), ((320, 256), F32), ((320, 256), F32),
    ((640, 256), F32), ((640, 1), F32), ((640, 1), F32), ((320, 256), F32), ((2, 320, 128), F32),
    ((4, 80, 256), F32), ((4, 80, 256), F32), ((2560, 768), BF16),
    ((320, 256), F32), ((2, 256, 256), BF16), ((2, 256, 256), BF16),
]
CONV_SEMS = (56, 56)
ATTEND_SEMS = (4, 4, 31, 31, 4, 4)


def encode_kernel(
    video_hbm, space_hbm, time_hbm, down_hbm, wq_hbm, wk_hbm, wv_hbm, wo_hbm, gain_ref, attn_gain_ref, out_ref,
    z_ref, wq_ref, wk_ref, wv_ref, wo_ref, load_sems, *scratch,
):
    c, a = len(CONV_SCRATCH), len(ATTEND_SCRATCH)
    conv_scratch, attend_scratch = scratch[:c], scratch[c : c + a]
    conv_sems, attend_sems = scratch[c + a : c + a + 2], scratch[c + a + 2 :]
    pairs = ((wq_hbm, wq_ref), (wk_hbm, wk_ref), (wv_hbm, wv_ref), (wo_hbm, wo_ref))
    loads = [pltpu.make_async_copy(src, dst, load_sems.at[4 + i]) for i, (src, dst) in enumerate(pairs)]
    greet, weights_ready, lowered_ready, attend = attend_part(
        attn_gain_ref, loads, wq_ref, wk_ref, wv_ref, wo_ref, z_ref, out_ref, *attend_scratch, *attend_sems
    )
    for load in loads:
        load.start()
    finish = conv_part(
        video_hbm, space_hbm, time_hbm, down_hbm, gain_ref, z_ref, *conv_scratch, *conv_sems,
        load_sems, greet, weights_ready, lowered_ready,
    )
    attend()
    finish()


def local(
    video,
    norm_gain,
    space_weight,
    time_weight,
    down_weight,
    attn_gain,
    w_query,
    w_key,
    w_value,
    w_out,
):
    vmem = pl.BlockSpec(memory_space=pltpu.VMEM)
    hbm = pl.BlockSpec(memory_space=pltpu.HBM)
    dma = pltpu.SemaphoreType.DMA
    square = pltpu.VMEM((256, 256), F32)
    return pl.pallas_call(
        encode_kernel,
        out_shape=jax.ShapeDtypeStruct((1, 320, 256), F32),
        in_specs=[hbm] * 8 + [vmem] * 2,
        out_specs=vmem,
        scratch_shapes=[
            pltpu.VMEM((4, 80, 256), F32), square, square, square, square, dma((8,)),
            *[pltpu.VMEM(shape, dtype) for shape, dtype in CONV_SCRATCH + ATTEND_SCRATCH],
            *[dma((count,)) for count in CONV_SEMS + ATTEND_SEMS],
        ],
        compiler_params=pltpu.CompilerParams(
            collective_id=3, has_side_effects=True, vmem_limit_bytes=56 * 2**20
        ),
        name="encode",
    )(
        video, space_weight.reshape(2, 1152, 128), time_weight.reshape(2, 384, 128), down_weight.reshape(1152, 256),
        w_query, w_key, w_value, w_out, norm_gain, attn_gain.reshape(1, 256),
    )


def solution(mesh):
    in_specs = (P("frame", "tile", None, None), P(), P(), P(), P(), P(), P(), P(), P(), P())
    out_specs = P(("frame", "tile"), None, None)
    return jax.shard_map(local, mesh=mesh, in_specs=in_specs, out_specs=out_specs, check_vma=False)
```

```python
import jax
import jax.numpy as jnp
from jax import lax
from jax.experimental import pallas as pl
from jax.experimental.pallas import tpu as pltpu
from jax.sharding import PartitionSpec as P

highest = lax.Precision.HIGHEST
MESH = pl.DeviceIdType.MESH
F32 = jnp.float32
BF16 = jnp.bfloat16


def norm(values, gain):
    return values * lax.rsqrt(jnp.mean(values * values, -1, keepdims=True) + 1e-06) * gain


def split(values):
    high = values.astype(BF16)
    return high, (values - high.astype(F32)).astype(BF16)


LEFT, RIGHT = 7, 48


def act(values, gain):
    scaled = values * lax.rsqrt(jnp.mean(values * values, -1, keepdims=True) + 1e-06) * gain
    return scaled / (1.0 + jnp.exp(-scaled))


def conv_part(
    video_hbm, space_hbm, time_hbm, down_hbm, gain_ref, z_ref,
    video_ref, space_ref, time_ref, down_ref,
    state, padded, ext, ext_in, cols, cols_in, corners, corners_in,
    late, late_in, u_hi, u_lo, a_hi, a_lo, d_hi, d_lo, w_space, w_time, w_hi, w_lo,
    send_sems, recv_sems, load_sems, greet, weights_ready, lowered_ready,
):
    tile = lax.axis_index("tile")
    frame = lax.axis_index("frame")
    loads = [
        pltpu.make_async_copy(video_hbm, video_ref, load_sems.at[0]),
        pltpu.make_async_copy(space_hbm, space_ref, load_sems.at[1]),
        pltpu.make_async_copy(time_hbm, time_ref, load_sems.at[2]),
        pltpu.make_async_copy(down_hbm, down_ref, load_sems.at[3]),
    ]
    for load in loads:
        load.start()
    k, z = tile // 4, tile % 4
    has_up, has_down = k > 0, k < 15
    has_left, has_right = z > 0, z < 3

    def dev(k, z, frame=frame):
        return {"tile": k * 4 + z, "frame": frame}

    def when(cond, fn):
        if cond is None:
            fn()
        else:
            pl.when(cond)(fn)

    ids = {}
    sent = []

    def message(name, src, dst, device):
        i = ids.setdefault(name, len(ids))
        return pltpu.make_async_remote_copy(
            src_ref=src, dst_ref=dst, send_sem=send_sems.at[i], recv_sem=recv_sems.at[i],
            device_id=device, device_id_type=MESH,
        )

    def start(name, src, dst, device, cond=None):
        copy = message(name, src, dst, device)
        when(cond, copy.start)
        sent.append((copy, cond))

    def arrived(name, ref, cond=None):
        copy = message(name, ref, ref, dev(k, (z + 1) % 4))
        when(cond, copy.wait_recv)

    for b in range(3):
        padded[b, :, :, 0:8, :] = jnp.zeros((4, 10, 8, 128), F32)
        padded[b, :, :, 48:56, :] = jnp.zeros((4, 10, 8, 128), F32)

        @pl.when(jnp.logical_not(has_up))
        def _():
            padded[b, :, 0, :, :] = jnp.zeros((4, 56, 128), F32)

        @pl.when(jnp.logical_not(has_down))
        def _():
            padded[b, :, 9, :, :] = jnp.zeros((4, 56, 128), F32)

    barrier = pltpu.get_barrier_semaphore()

    def hello(device, cond=None):
        when(cond, lambda: pl.semaphore_signal(barrier, inc=1, device_id=device, device_id_type=MESH))

    sides = ((-1, has_up), (1, has_down))
    flanks = ((-1, has_left), (1, has_right))
    for dz in range(1, 4):
        hello(dev(k, (z + dz) % 4))
    for dk, ok in sides:
        hello(dev((k + dk) % 16, z), ok)
        for dz, fine in flanks:
            hello(dev((k + dk) % 16, (z + dz) % 4), ok & fine)
    hello(dev(k, z, (frame + 3) % 4), frame > 0)
    count = 3 + (frame < 3).astype(jnp.int32)
    across = 1 + has_left.astype(jnp.int32) + has_right.astype(jnp.int32)
    count = count + (has_up.astype(jnp.int32) + has_down.astype(jnp.int32)) * across
    pl.semaphore_wait(barrier, count + greet(hello))

    order = (2, 3, 0, 1)

    def band(part):
        return pl.ds(pl.multiple_of(part * 40, 8), 40)

    def send_bands(fr):
        for dz in (1, 3, 2):
            part = (z + dz) % 4
            start(("band", fr, dz), video_hbm.at[fr, :, band(part), :], state.at[fr, pl.ds(z * 2, 2)], dev(k, part))
        bands = sent[-3:]
        del sent[-3:]
        return bands

    def bands_left(bands):
        for copy, _ in bands:
            copy.wait_send()

    bands = send_bands(2)
    loads[0].wait()
    for part in range(4):
        for fr in range(4):
            if part == 0:
                ext[part, fr, 0:2] = jnp.zeros((2, 1, 128), F32)
            else:
                ext[part, fr, 0:2] = video_ref[fr, :, 40 * part - 1 : 40 * part, :]
            if part == 3:
                ext[part, fr, 2:4] = jnp.zeros((2, 1, 128), F32)
            else:
                ext[part, fr, 2:4] = video_ref[fr, :, 40 * part + 40 : 40 * part + 41, :]

    for dz in (2, 1, 3):
        part = (z + dz) % 4
        start(("ext", dz), ext.at[part], ext_in.at[z], dev(k, part))
    ext_in[z] = ext[z]
    for fr in range(4):
        state[fr, pl.ds(z * 2, 2)] = video_ref[fr, :, band(z), :]

    bands_left(bands)
    bands = send_bands(3)

    for load in loads[1:]:
        load.wait()
    for b in range(2):
        for tap in range(9):
            rows = slice(tap * 128, tap * 128 + 128)
            high, low = split(space_ref[b, rows, :])
            w_space[b, rows, 0:128] = high
            w_space[b, rows, 128:256] = low
        high, low = split(time_ref[b])
        w_time[b, :, 0:128] = high
        w_time[b, :, 128:256] = low
    for tap in range(9):
        rows = slice(tap * 128, tap * 128 + 128)
        high, low = split(down_ref[rows, :])
        w_hi[rows, :] = high
        w_lo[rows, :] = low
    weights_ready()

    def two_part(high, low, weight):
        both = jnp.dot(high, weight, preferred_element_type=F32)
        rest = jnp.dot(low, weight[:, 0:128], preferred_element_type=F32)
        return both[:, 0:128] + both[:, 128:256] + rest

    inner = pl.ds(8, 40)

    def send_rows(b, f0, nf, width, both=True):
        f = pl.ds(f0, nf)
        start(("row", b, f0, 1), padded.at[b, f, 8, width, :], padded.at[b, f, 0, width, :], dev((k + 1) % 16, z), has_down)
        if both:
            start(("row", b, f0, -1), padded.at[b, f, 1, width, :], padded.at[b, f, 9, width, :], dev((k + 15) % 16, z), has_up)

    def rows_arrived(b, f0, nf, width, both=True):
        f = pl.ds(f0, nf)
        arrived(("row", b, f0, 1), padded.at[b, f, 0, width, :], has_up)
        if both:
            arrived(("row", b, f0, -1), padded.at[b, f, 9, width, :], has_down)

    def directions(both):
        return ((1, 1), (1, -1), (-1, 1), (-1, -1)) if both else ((1, 1),)

    def send_edges(b, f0, nf, both=True):
        f = pl.ds(f0, nf)
        for fr in range(f0, f0 + nf):
            cols[b - 1, 1, fr] = padded[b, fr, 1:9, 47:48, :]
            if both:
                cols[b - 1, 0, fr] = padded[b, fr, 1:9, 8:9, :]
            for dk, dz in directions(both):
                row, col = 8 if dk > 0 else 1, 47 if dz > 0 else 8
                corners[b - 1, (dk > 0) * 2 + (dz > 0), fr] = padded[b, fr, row, col : col + 1, :]
        start(("col", b, f0, 1), cols.at[b - 1, 1, f], cols_in.at[b - 1, 1, f], dev(k, (z + 1) % 4), has_right)
        if both:
            start(("col", b, f0, -1), cols.at[b - 1, 0, f], cols_in.at[b - 1, 0, f], dev(k, (z + 3) % 4), has_left)
        for dk, dz in directions(both):
            c = (dk > 0) * 2 + (dz > 0)
            ok = (has_down if dk > 0 else has_up) & (has_right if dz > 0 else has_left)
            start(
                ("corner", b, f0, dk, dz), corners.at[b - 1, c, f], corners_in.at[b - 1, c, f],
                dev((k + dk) % 16, (z + dz) % 4), ok,
            )

    def edges_arrived(b, f0, nf, both=True):
        f = pl.ds(f0, nf)
        rows_arrived(b, f0, nf, inner, both)
        arrived(("col", b, f0, 1), cols_in.at[b - 1, 1, f], has_left)
        if both:
            arrived(("col", b, f0, -1), cols_in.at[b - 1, 0, f], has_right)

        @pl.when(has_left)
        def _():
            for fr in range(f0, f0 + nf):
                padded[b, fr, 1:9, LEFT : LEFT + 1, :] = cols_in[b - 1, 1, fr]

        if both:
            @pl.when(has_right)
            def _():
                for fr in range(f0, f0 + nf):
                    padded[b, fr, 1:9, RIGHT : RIGHT + 1, :] = cols_in[b - 1, 0, fr]

        for dk, dz in directions(both):
            c = (dk > 0) * 2 + (dz > 0)
            ok = (has_up if dk > 0 else has_down) & (has_left if dz > 0 else has_right)
            arrived(("corner", b, f0, dk, dz), corners_in.at[b - 1, c, f], ok)

            @pl.when(ok)
            def _():
                row, col = 0 if dk > 0 else 9, LEFT if dz > 0 else RIGHT
                for fr in range(f0, f0 + nf):
                    padded[b, fr, row, col : col + 1, :] = corners_in[b - 1, c, fr]

    def conv(b, fr):
        at = fr % 2
        for dx in range(3):
            window = padded[b, fr, :, LEFT + dx : LEFT + dx + 40, :]
            for dy in range(3):
                lanes = slice((dy * 3 + dx) * 128, (dy * 3 + dx) * 128 + 128)
                high, low = split(window[dy : dy + 8].reshape(320, 128))
                a_hi[at, :, lanes] = high
                a_lo[at, :, lanes] = low
        mixed = two_part(a_hi[at], a_lo[at], w_space[b])
        u = act(mixed, gain_ref[b, 1:2, :])
        put(fr, u)
        if fr >= 2:
            late[b, fr - 2] = u
            start(
                ("late", b, fr), late.at[b, fr - 2], late_in.at[b, fr - 2],
                dev(k, z, (frame + 1) % 4), frame < 3,
            )

    def put(fr, u):
        lanes = slice((fr + 2) * 128, (fr + 3) * 128)
        u_hi[:, lanes], u_lo[:, lanes] = split(u)

    def earlier(b):
        for fr in (2, 3):
            arrived(("late", b, fr), late_in.at[b, fr - 2], frame > 0)

        @pl.when(frame > 0)
        def _():
            put(-2, late_in[b, 0])
            put(-1, late_in[b, 1])

        @pl.when(frame == 0)
        def _():
            for parts in (u_hi, u_lo):
                parts[:, 0:128] = parts[:, 256:384]
                parts[:, 128:256] = parts[:, 256:384]

    def mix(b, fr):
        lanes = slice(fr * 128, fr * 128 + 384)
        return state[fr].reshape(320, 128) + two_part(u_hi[:, lanes], u_lo[:, lanes], w_time[b])

    bands_left(bands)
    sent.extend(send_bands(0))

    for dz in range(1, 4):
        arrived(("ext", dz), ext_in.at[(z + dz) % 4])
    gain = gain_ref[0, 0:1, :]
    for fr in order:
        if fr == 3:
            sent.extend(send_bands(1))
        for dz in range(1, 4):
            arrived(("band", fr, dz), state.at[fr, pl.ds(((z + dz) % 4) * 2, 2)])
        padded[0, fr, 1:9, 8:48, :] = act(state[fr].reshape(320, 128), gain).reshape(8, 40, 128)
        for src in range(4):
            fringe = act(ext_in[src, fr], gain)
            rows = slice(1 + 2 * src, 3 + 2 * src)

            @pl.when(has_left)
            def _():
                padded[0, fr, rows, LEFT : LEFT + 1, :] = fringe[0:2]

            @pl.when(has_right)
            def _():
                padded[0, fr, rows, RIGHT : RIGHT + 1, :] = fringe[2:4]
        send_rows(0, fr, 1, slice(None))
        if fr < 2:
            rows_arrived(0, fr + 2, 1, slice(None))
            conv(0, fr + 2)
    for fr in (0, 1):
        rows_arrived(0, fr, 1, slice(None))
        conv(0, fr)

    gain = gain_ref[1, 0:1, :]

    def middle(f0):
        for fr in (f0, f0 + 1):
            x = mix(0, fr)
            padded[1, fr, 1:9, 8:48, :] = act(x, gain).reshape(8, 40, 128)
            state[fr] = x.reshape(8, 40, 128)
        send_rows(1, f0, 2, inner)
        send_edges(1, f0, 2)

    middle(2)
    earlier(0)
    middle(0)
    for f0 in (2, 0):
        edges_arrived(1, f0, 2)
        for fr in (f0, f0 + 1):
            conv(1, fr)
    for f0 in (2, 0):
        if f0 == 0:
            earlier(1)
        for fr in (f0, f0 + 1):
            padded[2, fr, 1:9, 8:48, :] = mix(1, fr).reshape(8, 40, 128)
        send_rows(2, f0, 2, inner, False)
        send_edges(2, f0, 2, False)

    def take(f0, row, dy, dx):
        lanes = slice((dy * 3 + dx) * 128, (dy * 3 + dx) * 128 + 128)
        for fr in (f0, f0 + 1):
            at = slice((fr - f0) * 96 + row * 24, (fr - f0) * 96 + row * 24 + 24)
            taken = padded[2, fr, 2 * row + dy, pl.ds(LEFT + dx, 24, stride=2), :]
            high = taken.astype(BF16).astype(F32)
            d_hi[at, lanes] = high
            d_lo[at, lanes] = taken - high

    taps = [(row, dy, dx) for row in range(4) for dy in range(3) for dx in range(3)]
    for f0 in (2, 0):
        for row, dy, dx in taps:
            if dx > 0 and row + dy > 0:
                take(f0, row, dy, dx)
        edges_arrived(2, f0, 2, False)
        for row, dy, dx in taps:
            if dx == 0 or row + dy == 0:
                take(f0, row, dy, dx)
        high, low = d_hi[...].astype(BF16), d_lo[...].astype(BF16)
        lowered = jnp.dot(high, w_hi[...], preferred_element_type=F32)
        lowered = lowered + jnp.dot(high, w_lo[...], preferred_element_type=F32)
        lowered = lowered + jnp.dot(low, w_hi[...], preferred_element_type=F32)
        for fr in (f0, f0 + 1):
            for row in range(4):
                for part in range(4):
                    at = (fr - f0) * 96 + row * 24 + part * 5
                    z_ref[fr, part * 20 + row * 5 : part * 20 + row * 5 + 5, :] = lowered[at : at + 5]
            lowered_ready(fr)

    def finish():
        for copy, cond in sent:
            when(cond, copy.wait_send)

    return finish


def dot_f32(a, b, dims=((1,), (0,))):
    return lax.dot_general(a, b, (dims, ((), ())), precision=highest, preferred_element_type=F32)


def attend_part(
    gain_ref, loads, wq_ref, wk_ref, wv_ref, wo_ref, z_ref, out_ref,
    keys, q_ref, q_own, q_in, acc, best, total, part_acc, part_stat, result, landing, k_ref, own_z, w_qk, w_vo,
    s1, r1, ss, rs, rets, retr,
):
    tile = lax.axis_index("tile")
    frame = lax.axis_index("frame")
    x, y, z = tile // 16, (tile // 4) % 4, tile % 4
    half, s = z // 2, z % 2
    zh, core = frame // 2, frame % 2

    def dev(x, y, z, core):
        return {"tile": x * 16 + y * 4 + z, "frame": zh * 2 + core}

    up = dev(x, (y + 1) % 4, z, core)
    down = dev(x, (y + 3) % 4, z, core)
    mate = dev(x, y, z + 1 - 2 * s, core)
    sibling = dev(x, y, z, 1 - core)
    sz = 2 * core + s
    crossed = half != core
    uncrossed = jnp.logical_not(crossed)

    from_z, from_core = 2 * core + y % 2, y // 2

    def greet(hello):
        for device in (up, down, mate, sibling):
            hello(device)
        for dx in range(1, 4):
            hello(dev((x + dx) % 4, y, sz, half))
        hello(dev(x, y, sz, half), crossed)
        expected = 7 + crossed.astype(jnp.int32)
        for j in range(4):
            hello(
                dev(x, j, from_z, from_core),
                jnp.logical_not((j == y) & (from_z == z) & (from_core == core)),
            )
            expected = expected + jnp.logical_not((sz == y) & (z == j) & (half == core)).astype(jnp.int32)
        return expected

    slot = s * 4 + y

    def block(b):
        return pl.ds(b * 80, 80)

    mine = pl.ds(pl.multiple_of(x * 80, 80), 80)

    def to_group(fr):
        return pltpu.make_async_remote_copy(
            src_ref=z_ref.at[fr],
            dst_ref=own_z.at[mine],
            send_sem=s1.at[fr],
            recv_sem=r1.at[x],
            device_id=dev(fr, y, sz, half),
            device_id_type=MESH,
        )

    def lowered_ready(fr):
        stays = uncrossed & (x == fr)

        @pl.when(jnp.logical_not(stays))
        def _():
            to_group(fr).start()

        @pl.when(stays)
        def _():
            own_z[mine, :] = z_ref[fr]

    def weights_ready():
        for load in loads:
            load.wait()
        together = dot_f32(wq_ref[...], wk_ref[...], ((1,), (1,))) * (256.0 ** -0.5 * 1.4426950408889634)
        w_qk[0], w_qk[1] = split(together)
        w_vo[0], w_vo[1] = split(dot_f32(wv_ref[...], wo_ref[...]))

    def three_part(values, weight):
        high, low = split(values)
        total = jnp.dot(high, weight[0], preferred_element_type=F32)
        total = total + jnp.dot(high, weight[1], preferred_element_type=F32)
        return total + jnp.dot(low, weight[0], preferred_element_type=F32)

    def run():
        sent = []
        slot_up = s * 4 + (y + 1) % 4
        slot_down = s * 4 + (y + 3) % 4
        slot_far = s * 4 + (y + 2) % 4
        other = (1 - s) * 4
        mate_own, mate_up = other + y, other + (y + 1) % 4
        mate_down, mate_far = other + (y + 3) % 4, other + (y + 2) % 4

        def remote(src, dst, device, i):
            return pltpu.make_async_remote_copy(
                src_ref=src, dst_ref=dst, send_sem=ss.at[i], recv_sem=rs.at[i],
                device_id=device, device_id_type=MESH,
            )

        own_up, own_down, own_mate, mate_goes_up, mate_goes_down, far_on, far_mate = range(7)

        def push(kind, b, source, device):
            ref = keys.at[source, block(b)]
            copy = remote(ref, ref, device, kind * 4 + b)
            copy.start()
            sent.append(copy)

        def landed(kind, b, source):
            ref = keys.at[source, block(b)]
            remote(ref, ref, sibling, kind * 4 + b).wait_recv()

        gain = gain_ref[...]
        for b in range(4):
            @pl.when(jnp.logical_not(uncrossed & (x == b)))
            def _():
                pltpu.make_async_remote_copy(
                    src_ref=z_ref.at[0],
                    dst_ref=own_z.at[block(b)],
                    send_sem=s1.at[b],
                    recv_sem=r1.at[b],
                    device_id=sibling,
                    device_id_type=MESH,
                ).wait_recv()

            keys[slot, block(b), :] = norm(own_z[block(b)], gain)
            push(own_up, b, slot, up)
            push(own_down, b, slot, down)
            push(own_mate, b, slot, mate)
        def place_query(at, values):
            rows = slice(at, at + 320)
            high, low = split(values[...])
            q_ref[rows, 0:256] = high
            q_ref[rows, 256:512] = low
            q_ref[rows, 512:768] = high

        q_own[...] = three_part(keys[slot], w_qk)
        q_copy = remote(q_own, q_in, sibling, 28)
        q_copy.start()
        sent.append(q_copy)
        place_query(0, q_own)

        best[...] = jnp.full_like(best, -jnp.inf)
        total[...] = jnp.zeros_like(total)
        acc[...] = jnp.zeros_like(acc)

        def product(a, b, dims):
            return lax.dot_general(a, b, (dims, ((), ())), preferred_element_type=F32)

        def prepare(at, source):
            place = slice(at * 320, at * 320 + 320)
            high, low = split(keys[source])
            k_ref[place, 0:256] = high
            k_ref[place, 256:512] = high
            k_ref[place, 512:768] = low

        def attend(start, stop, rows):
            place = slice(start * 320, stop * 320)
            k_hi, k_lo = k_ref[place, 0:256], k_ref[place, 512:768]
            scores = product(q_ref[rows], k_ref[place], ((1,), (1,)))
            old = best[rows]
            new = jnp.maximum(old, jnp.max(scores, axis=1, keepdims=True))
            factor = jnp.exp2(old - new)
            weights = jnp.exp2(scores - new)
            total[rows] = total[rows] * factor + jnp.sum(weights, axis=1, keepdims=True)
            best[rows] = new
            p_hi, p_lo = split(weights)
            along = ((1,), (0,))
            mixed = product(p_hi, k_hi, along) + product(p_hi, k_lo, along) + product(p_lo, k_hi, along)
            acc[rows] = acc[rows] * factor + mixed

        first, second = slice(0, 320), slice(320, 640)

        def forward(b):
            if b < 2:
                landed(own_up, b, slot_down)
                push(far_on, b, slot_down, up)
                landed(own_down, b, slot_up)
            else:
                landed(own_down, b, slot_up)
                push(far_on, b, slot_up, down)
                landed(own_up, b, slot_down)
            landed(own_mate, b, mate_own)
            push(mate_goes_up, b, mate_own, up)
            push(mate_goes_down, b, mate_own, down)

        def far_forward(b):
            landed(far_on, b, slot_far)
            push(far_mate, b, slot_far, mate)

        forward(0)
        prepare(0, slot)
        attend(0, 1, first)
        forward(1)
        q_copy.wait_recv()
        place_query(320, q_in)
        attend(0, 1, second)
        forward(2)
        forward(3)
        prepare(1, slot_down)
        far_forward(0)
        prepare(2, slot_up)
        far_forward(1)
        far_forward(2)
        prepare(3, mate_own)
        far_forward(3)
        prepare(4, slot_far)
        attend(1, 5, second)
        attend(1, 5, first)
        for b in range(4):
            landed(mate_goes_up, b, mate_down)
        prepare(5, mate_down)
        for b in range(4):
            landed(mate_goes_down, b, mate_up)
        prepare(6, mate_up)
        for b in range(4):
            landed(far_mate, b, mate_far)
        prepare(7, mate_far)
        attend(5, 8, second)
        part_stat[0, :, 0:64] = jnp.broadcast_to(best[second], (320, 64))
        part_stat[0, :, 64:128] = jnp.broadcast_to(total[second], (320, 64))
        merge = [
            remote(part_stat.at[0], part_stat.at[1], sibling, 30),
            remote(acc.at[pl.ds(320, 320)], part_acc, sibling, 29),
        ]
        for copy in merge:
            copy.start()
        attend(5, 8, first)
        for copy in merge:
            copy.wait_recv()
        sent.extend(merge)
        other_best = part_stat[1, :, 0:1]
        other_total = part_stat[1, :, 64:65]
        top = jnp.maximum(best[first], other_best)
        mine_f = jnp.exp2(best[first] - top)
        other_f = jnp.exp2(other_best - top)
        whole = total[first] * mine_f + other_total * other_f
        mixed = (acc[first] * mine_f + part_acc[...] * other_f) / whole
        y_out = own_z[...] + three_part(mixed, w_vo)

        backs = []
        for part in range(4):
            for b in range(4):
                start = b * 80 + part * 20
                result[part, b * 20 : b * 20 + 20] = y_out[start : start + 20]
            copy = pltpu.make_async_remote_copy(
                src_ref=result.at[part],
                dst_ref=landing.at[y],
                send_sem=rets.at[part],
                recv_sem=retr.at[y],
                device_id=dev(x, sz, part, half),
                device_id_type=MESH,
            )
            stays = (sz == y) & (z == part) & (half == core)
            backs.append((copy, stays))

            @pl.when(jnp.logical_not(stays))
            def _():
                copy.start()

            @pl.when(stays)
            def _():
                landing[y] = result[part]

        for sy in range(4):
            here = (sy == y) & (from_z == z) & (from_core == core)

            @pl.when(jnp.logical_not(here))
            def _():
                pltpu.make_async_remote_copy(
                    src_ref=result.at[0],
                    dst_ref=landing.at[sy],
                    send_sem=rets.at[0],
                    recv_sem=retr.at[sy],
                    device_id=sibling,
                    device_id_type=MESH,
                ).wait_recv()

            for sx in range(4):
                at = (sx * 4 + sy) * 20
                out_ref[0, at : at + 20, :] = landing[sy, sx * 20 : sx * 20 + 20]

        for fr in range(4):
            @pl.when(jnp.logical_not(uncrossed & (x == fr)))
            def _():
                to_group(fr).wait_send()

        for copy in sent:
            copy.wait_send()
        for copy, stays in backs:
            @pl.when(jnp.logical_not(stays))
            def _():
                copy.wait_send()

    return greet, weights_ready, lowered_ready, run


CONV_SCRATCH = [
    ((4, 2, 160, 128), F32), ((2, 1152, 128), F32), ((2, 384, 128), F32), ((1152, 256), F32),
    ((4, 8, 40, 128), F32), ((3, 4, 10, 56, 128), F32), ((4, 4, 4, 1, 128), F32), ((4, 4, 4, 1, 128), F32),
    ((2, 2, 4, 8, 1, 128), F32), ((2, 2, 4, 8, 1, 128), F32), ((2, 4, 4, 1, 128), F32), ((2, 4, 4, 1, 128), F32),
    ((2, 2, 320, 128), F32), ((2, 2, 320, 128), F32), ((320, 768), BF16), ((320, 768), BF16),
    ((2, 320, 1152), BF16), ((2, 320, 1152), BF16), ((192, 1152), F32), ((192, 1152), F32),
    ((2, 1152, 256), BF16), ((2, 384, 256), BF16), ((1152, 256), BF16), ((1152, 256), BF16),
]
ATTEND_SCRATCH = [
    ((8, 320, 256), F32), ((640, 768), BF16), ((320, 256), F32), ((320, 256), F32),
    ((640, 256), F32), ((640, 1), F32), ((640, 1), F32), ((320, 256), F32), ((2, 320, 128), F32),
    ((4, 80, 256), F32), ((4, 80, 256), F32), ((2560, 768), BF16),
    ((320, 256), F32), ((2, 256, 256), BF16), ((2, 256, 256), BF16),
]
CONV_SEMS = (56, 56)
ATTEND_SEMS = (4, 4, 31, 31, 4, 4)


def encode_kernel(
    video_hbm, space_hbm, time_hbm, down_hbm, wq_hbm, wk_hbm, wv_hbm, wo_hbm, gain_ref, attn_gain_ref, out_ref,
    z_ref, wq_ref, wk_ref, wv_ref, wo_ref, load_sems, *scratch,
):
    c, a = len(CONV_SCRATCH), len(ATTEND_SCRATCH)
    conv_scratch, attend_scratch = scratch[:c], scratch[c : c + a]
    conv_sems, attend_sems = scratch[c + a : c + a + 2], scratch[c + a + 2 :]
    pairs = ((wq_hbm, wq_ref), (wk_hbm, wk_ref), (wv_hbm, wv_ref), (wo_hbm, wo_ref))
    loads = [pltpu.make_async_copy(src, dst, load_sems.at[4 + i]) for i, (src, dst) in enumerate(pairs)]
    greet, weights_ready, lowered_ready, attend = attend_part(
        attn_gain_ref, loads, wq_ref, wk_ref, wv_ref, wo_ref, z_ref, out_ref, *attend_scratch, *attend_sems
    )
    for load in loads:
        load.start()
    finish = conv_part(
        video_hbm, space_hbm, time_hbm, down_hbm, gain_ref, z_ref, *conv_scratch, *conv_sems,
        load_sems, greet, weights_ready, lowered_ready,
    )
    attend()
    finish()


def local(
    video,
    norm_gain,
    space_weight,
    time_weight,
    down_weight,
    attn_gain,
    w_query,
    w_key,
    w_value,
    w_out,
):
    vmem = pl.BlockSpec(memory_space=pltpu.VMEM)
    hbm = pl.BlockSpec(memory_space=pltpu.HBM)
    dma = pltpu.SemaphoreType.DMA
    square = pltpu.VMEM((256, 256), F32)
    return pl.pallas_call(
        encode_kernel,
        out_shape=jax.ShapeDtypeStruct((1, 320, 256), F32),
        in_specs=[hbm] * 8 + [vmem] * 2,
        out_specs=vmem,
        scratch_shapes=[
            pltpu.VMEM((4, 80, 256), F32), square, square, square, square, dma((8,)),
            *[pltpu.VMEM(shape, dtype) for shape, dtype in CONV_SCRATCH + ATTEND_SCRATCH],
            *[dma((count,)) for count in CONV_SEMS + ATTEND_SEMS],
        ],
        compiler_params=pltpu.CompilerParams(
            collective_id=3, has_side_effects=True, vmem_limit_bytes=56 * 2**20
        ),
        name="encode",
    )(
        video, space_weight.reshape(2, 1152, 128), time_weight.reshape(2, 384, 128), down_weight.reshape(1152, 256),
        w_query, w_key, w_value, w_out, norm_gain, attn_gain.reshape(1, 256),
    )


def solution(mesh):
    in_specs = (P("frame", "tile", None, None), P(), P(), P(), P(), P(), P(), P(), P(), P())
    out_specs = P(("frame", "tile"), None, None)
    return jax.shard_map(local, mesh=mesh, in_specs=in_specs, out_specs=out_specs, check_vma=False)
```

```python
import jax
import jax.numpy as jnp
from jax import lax
from jax.experimental import pallas as pl
from jax.experimental.pallas import tpu as pltpu
from jax.sharding import PartitionSpec as P

highest = lax.Precision.HIGHEST
MESH = pl.DeviceIdType.MESH
F32 = jnp.float32
BF16 = jnp.bfloat16


def norm(values, gain):
    return values * lax.rsqrt(jnp.mean(values * values, -1, keepdims=True) + 1e-06) * gain


def split(values):
    high = values.astype(BF16)
    return high, (values - high.astype(F32)).astype(BF16)


LEFT, RIGHT = 7, 48


def act(values, gain):
    scaled = values * lax.rsqrt(jnp.mean(values * values, -1, keepdims=True) + 1e-06) * gain
    return scaled / (1.0 + jnp.exp(-scaled))


def conv_part(
    video_hbm, space_hbm, time_hbm, down_hbm, gain_ref, z_ref,
    video_ref, space_ref, time_ref, down_ref,
    state, padded, ext, ext_in, cols, cols_in, corners, corners_in,
    late, late_in, u_hi, u_lo, a_hi, a_lo, d_hi, d_lo, w_space, w_time, w_hi, w_lo,
    send_sems, recv_sems, load_sems, greet, weights_ready, lowered_ready,
):
    tile = lax.axis_index("tile")
    frame = lax.axis_index("frame")
    loads = [
        pltpu.make_async_copy(video_hbm, video_ref, load_sems.at[0]),
        pltpu.make_async_copy(space_hbm, space_ref, load_sems.at[1]),
        pltpu.make_async_copy(time_hbm, time_ref, load_sems.at[2]),
        pltpu.make_async_copy(down_hbm, down_ref, load_sems.at[3]),
    ]
    for load in loads:
        load.start()
    k, z = tile // 4, tile % 4
    has_up, has_down = k > 0, k < 15
    has_left, has_right = z > 0, z < 3

    def dev(k, z, frame=frame):
        return {"tile": k * 4 + z, "frame": frame}

    def when(cond, fn):
        if cond is None:
            fn()
        else:
            pl.when(cond)(fn)

    ids = {}
    sent = []

    def message(name, src, dst, device):
        i = ids.setdefault(name, len(ids))
        return pltpu.make_async_remote_copy(
            src_ref=src, dst_ref=dst, send_sem=send_sems.at[i], recv_sem=recv_sems.at[i],
            device_id=device, device_id_type=MESH,
        )

    def start(name, src, dst, device, cond=None):
        copy = message(name, src, dst, device)
        when(cond, copy.start)
        sent.append((copy, cond))

    def arrived(name, ref, cond=None):
        copy = message(name, ref, ref, dev(k, (z + 1) % 4))
        when(cond, copy.wait_recv)

    for b in range(3):
        padded[b, :, :, 0:8, :] = jnp.zeros((4, 10, 8, 128), F32)
        padded[b, :, :, 48:56, :] = jnp.zeros((4, 10, 8, 128), F32)

        @pl.when(jnp.logical_not(has_up))
        def _():
            padded[b, :, 0, :, :] = jnp.zeros((4, 56, 128), F32)

        @pl.when(jnp.logical_not(has_down))
        def _():
            padded[b, :, 9, :, :] = jnp.zeros((4, 56, 128), F32)

    barrier = pltpu.get_barrier_semaphore()

    def hello(device, cond=None):
        when(cond, lambda: pl.semaphore_signal(barrier, inc=1, device_id=device, device_id_type=MESH))

    sides = ((-1, has_up), (1, has_down))
    flanks = ((-1, has_left), (1, has_right))
    for dz in range(1, 4):
        hello(dev(k, (z + dz) % 4))
    for dk, ok in sides:
        hello(dev((k + dk) % 16, z), ok)
        for dz, fine in flanks:
            hello(dev((k + dk) % 16, (z + dz) % 4), ok & fine)
    hello(dev(k, z, (frame + 3) % 4), frame > 0)
    count = 3 + (frame < 3).astype(jnp.int32)
    across = 1 + has_left.astype(jnp.int32) + has_right.astype(jnp.int32)
    count = count + (has_up.astype(jnp.int32) + has_down.astype(jnp.int32)) * across
    pl.semaphore_wait(barrier, count + greet(hello))

    order = (2, 3, 0, 1)

    def band(part):
        return pl.ds(pl.multiple_of(part * 40, 8), 40)

    def send_bands(fr):
        for dz in (1, 3, 2):
            part = (z + dz) % 4
            start(("band", fr, dz), video_hbm.at[fr, :, band(part), :], state.at[fr, pl.ds(z * 2, 2)], dev(k, part))
        bands = sent[-3:]
        del sent[-3:]
        return bands

    def bands_left(bands):
        for copy, _ in bands:
            copy.wait_send()

    bands = send_bands(2)
    loads[0].wait()
    for part in range(4):
        for fr in range(4):
            if part == 0:
                ext[part, fr, 0:2] = jnp.zeros((2, 1, 128), F32)
            else:
                ext[part, fr, 0:2] = video_ref[fr, :, 40 * part - 1 : 40 * part, :]
            if part == 3:
                ext[part, fr, 2:4] = jnp.zeros((2, 1, 128), F32)
            else:
                ext[part, fr, 2:4] = video_ref[fr, :, 40 * part + 40 : 40 * part + 41, :]

    for dz in (2, 1, 3):
        part = (z + dz) % 4
        start(("ext", dz), ext.at[part], ext_in.at[z], dev(k, part))
    ext_in[z] = ext[z]
    for fr in range(4):
        state[fr, pl.ds(z * 2, 2)] = video_ref[fr, :, band(z), :]

    bands_left(bands)
    bands = send_bands(3)

    for load in loads[1:]:
        load.wait()
    for b in range(2):
        for tap in range(9):
            rows = slice(tap * 128, tap * 128 + 128)
            high, low = split(space_ref[b, rows, :])
            w_space[b, rows, 0:128] = high
            w_space[b, rows, 128:256] = low
        high, low = split(time_ref[b])
        w_time[b, :, 0:128] = high
        w_time[b, :, 128:256] = low
    for tap in range(9):
        rows = slice(tap * 128, tap * 128 + 128)
        high, low = split(down_ref[rows, :])
        w_hi[rows, :] = high
        w_lo[rows, :] = low
    weights_ready()

    def two_part(high, low, weight):
        both = jnp.dot(high, weight, preferred_element_type=F32)
        rest = jnp.dot(low, weight[:, 0:128], preferred_element_type=F32)
        return both[:, 0:128] + both[:, 128:256] + rest

    inner = pl.ds(8, 40)

    def send_rows(b, f0, nf, width, both=True):
        f = pl.ds(f0, nf)
        start(("row", b, f0, 1), padded.at[b, f, 8, width, :], padded.at[b, f, 0, width, :], dev((k + 1) % 16, z), has_down)
        if both:
            start(("row", b, f0, -1), padded.at[b, f, 1, width, :], padded.at[b, f, 9, width, :], dev((k + 15) % 16, z), has_up)

    def rows_arrived(b, f0, nf, width, both=True):
        f = pl.ds(f0, nf)
        arrived(("row", b, f0, 1), padded.at[b, f, 0, width, :], has_up)
        if both:
            arrived(("row", b, f0, -1), padded.at[b, f, 9, width, :], has_down)

    def directions(both):
        return ((1, 1), (1, -1), (-1, 1), (-1, -1)) if both else ((1, 1),)

    def send_edges(b, f0, nf, both=True):
        f = pl.ds(f0, nf)
        for fr in range(f0, f0 + nf):
            cols[b - 1, 1, fr] = padded[b, fr, 1:9, 47:48, :]
            if both:
                cols[b - 1, 0, fr] = padded[b, fr, 1:9, 8:9, :]
            for dk, dz in directions(both):
                row, col = 8 if dk > 0 else 1, 47 if dz > 0 else 8
                corners[b - 1, (dk > 0) * 2 + (dz > 0), fr] = padded[b, fr, row, col : col + 1, :]
        start(("col", b, f0, 1), cols.at[b - 1, 1, f], cols_in.at[b - 1, 1, f], dev(k, (z + 1) % 4), has_right)
        if both:
            start(("col", b, f0, -1), cols.at[b - 1, 0, f], cols_in.at[b - 1, 0, f], dev(k, (z + 3) % 4), has_left)
        for dk, dz in directions(both):
            c = (dk > 0) * 2 + (dz > 0)
            ok = (has_down if dk > 0 else has_up) & (has_right if dz > 0 else has_left)
            start(
                ("corner", b, f0, dk, dz), corners.at[b - 1, c, f], corners_in.at[b - 1, c, f],
                dev((k + dk) % 16, (z + dz) % 4), ok,
            )

    def edges_arrived(b, f0, nf, both=True):
        f = pl.ds(f0, nf)
        rows_arrived(b, f0, nf, inner, both)
        arrived(("col", b, f0, 1), cols_in.at[b - 1, 1, f], has_left)
        if both:
            arrived(("col", b, f0, -1), cols_in.at[b - 1, 0, f], has_right)

        @pl.when(has_left)
        def _():
            for fr in range(f0, f0 + nf):
                padded[b, fr, 1:9, LEFT : LEFT + 1, :] = cols_in[b - 1, 1, fr]

        if both:
            @pl.when(has_right)
            def _():
                for fr in range(f0, f0 + nf):
                    padded[b, fr, 1:9, RIGHT : RIGHT + 1, :] = cols_in[b - 1, 0, fr]

        for dk, dz in directions(both):
            c = (dk > 0) * 2 + (dz > 0)
            ok = (has_up if dk > 0 else has_down) & (has_left if dz > 0 else has_right)
            arrived(("corner", b, f0, dk, dz), corners_in.at[b - 1, c, f], ok)

            @pl.when(ok)
            def _():
                row, col = 0 if dk > 0 else 9, LEFT if dz > 0 else RIGHT
                for fr in range(f0, f0 + nf):
                    padded[b, fr, row, col : col + 1, :] = corners_in[b - 1, c, fr]

    def conv(b, fr):
        at = fr % 2
        for dx in range(3):
            window = padded[b, fr, :, LEFT + dx : LEFT + dx + 40, :]
            for dy in range(3):
                lanes = slice((dy * 3 + dx) * 128, (dy * 3 + dx) * 128 + 128)
                high, low = split(window[dy : dy + 8].reshape(320, 128))
                a_hi[at, :, lanes] = high
                a_lo[at, :, lanes] = low
        mixed = two_part(a_hi[at], a_lo[at], w_space[b])
        u = act(mixed, gain_ref[b, 1:2, :])
        put(fr, u)
        if fr >= 2:
            late[b, fr - 2] = u
            start(
                ("late", b, fr), late.at[b, fr - 2], late_in.at[b, fr - 2],
                dev(k, z, (frame + 1) % 4), frame < 3,
            )

    def put(fr, u):
        lanes = slice((fr + 2) * 128, (fr + 3) * 128)
        u_hi[:, lanes], u_lo[:, lanes] = split(u)

    def earlier(b):
        for fr in (2, 3):
            arrived(("late", b, fr), late_in.at[b, fr - 2], frame > 0)

        @pl.when(frame > 0)
        def _():
            put(-2, late_in[b, 0])
            put(-1, late_in[b, 1])

        @pl.when(frame == 0)
        def _():
            for parts in (u_hi, u_lo):
                parts[:, 0:128] = parts[:, 256:384]
                parts[:, 128:256] = parts[:, 256:384]

    def mix(b, fr):
        lanes = slice(fr * 128, fr * 128 + 384)
        return state[fr].reshape(320, 128) + two_part(u_hi[:, lanes], u_lo[:, lanes], w_time[b])

    bands_left(bands)
    bands = send_bands(0)

    for dz in range(1, 4):
        arrived(("ext", dz), ext_in.at[(z + dz) % 4])
    gain = gain_ref[0, 0:1, :]
    for fr in order:
        if fr == 0:
            bands_left(bands)
            sent.extend(send_bands(1))
        for dz in range(1, 4):
            arrived(("band", fr, dz), state.at[fr, pl.ds(((z + dz) % 4) * 2, 2)])
        padded[0, fr, 1:9, 8:48, :] = act(state[fr].reshape(320, 128), gain).reshape(8, 40, 128)
        for src in range(4):
            fringe = act(ext_in[src, fr], gain)
            rows = slice(1 + 2 * src, 3 + 2 * src)

            @pl.when(has_left)
            def _():
                padded[0, fr, rows, LEFT : LEFT + 1, :] = fringe[0:2]

            @pl.when(has_right)
            def _():
                padded[0, fr, rows, RIGHT : RIGHT + 1, :] = fringe[2:4]
        send_rows(0, fr, 1, slice(None))
        if fr < 2:
            rows_arrived(0, fr + 2, 1, slice(None))
            conv(0, fr + 2)
    for fr in (0, 1):
        rows_arrived(0, fr, 1, slice(None))
        conv(0, fr)

    gain = gain_ref[1, 0:1, :]

    def middle(f0):
        for fr in (f0, f0 + 1):
            x = mix(0, fr)
            padded[1, fr, 1:9, 8:48, :] = act(x, gain).reshape(8, 40, 128)
            state[fr] = x.reshape(8, 40, 128)
        send_rows(1, f0, 2, inner)
        send_edges(1, f0, 2)

    middle(2)
    earlier(0)
    middle(0)
    for f0 in (2, 0):
        edges_arrived(1, f0, 2)
        for fr in (f0, f0 + 1):
            conv(1, fr)
    for f0 in (2, 0):
        if f0 == 0:
            earlier(1)
        for fr in (f0, f0 + 1):
            padded[2, fr, 1:9, 8:48, :] = mix(1, fr).reshape(8, 40, 128)
        send_rows(2, f0, 2, inner, False)
        send_edges(2, f0, 2, False)

    def take(f0, row, dy, dx):
        lanes = slice((dy * 3 + dx) * 128, (dy * 3 + dx) * 128 + 128)
        for fr in (f0, f0 + 1):
            at = slice((fr - f0) * 96 + row * 24, (fr - f0) * 96 + row * 24 + 24)
            taken = padded[2, fr, 2 * row + dy, pl.ds(LEFT + dx, 24, stride=2), :]
            high = taken.astype(BF16).astype(F32)
            d_hi[at, lanes] = high
            d_lo[at, lanes] = taken - high

    taps = [(row, dy, dx) for row in range(4) for dy in range(3) for dx in range(3)]
    for f0 in (2, 0):
        for row, dy, dx in taps:
            if dx > 0 and row + dy > 0:
                take(f0, row, dy, dx)
        edges_arrived(2, f0, 2, False)
        for row, dy, dx in taps:
            if dx == 0 or row + dy == 0:
                take(f0, row, dy, dx)
        high, low = d_hi[...].astype(BF16), d_lo[...].astype(BF16)
        lowered = jnp.dot(high, w_hi[...], preferred_element_type=F32)
        lowered = lowered + jnp.dot(high, w_lo[...], preferred_element_type=F32)
        lowered = lowered + jnp.dot(low, w_hi[...], preferred_element_type=F32)
        for fr in (f0, f0 + 1):
            for row in range(4):
                for part in range(4):
                    at = (fr - f0) * 96 + row * 24 + part * 5
                    z_ref[fr, part * 20 + row * 5 : part * 20 + row * 5 + 5, :] = lowered[at : at + 5]
            lowered_ready(fr)

    def finish():
        for copy, cond in sent:
            when(cond, copy.wait_send)

    return finish


def dot_f32(a, b, dims=((1,), (0,))):
    return lax.dot_general(a, b, (dims, ((), ())), precision=highest, preferred_element_type=F32)


def attend_part(
    gain_ref, loads, wq_ref, wk_ref, wv_ref, wo_ref, z_ref, out_ref,
    keys, q_ref, q_own, q_in, acc, best, total, part_acc, part_stat, result, landing, k_ref, own_z, w_qk, w_vo,
    s1, r1, ss, rs, rets, retr,
):
    tile = lax.axis_index("tile")
    frame = lax.axis_index("frame")
    x, y, z = tile // 16, (tile // 4) % 4, tile % 4
    half, s = z // 2, z % 2
    zh, core = frame // 2, frame % 2

    def dev(x, y, z, core):
        return {"tile": x * 16 + y * 4 + z, "frame": zh * 2 + core}

    up = dev(x, (y + 1) % 4, z, core)
    down = dev(x, (y + 3) % 4, z, core)
    mate = dev(x, y, z + 1 - 2 * s, core)
    sibling = dev(x, y, z, 1 - core)
    sz = 2 * core + s
    crossed = half != core
    uncrossed = jnp.logical_not(crossed)

    from_z, from_core = 2 * core + y % 2, y // 2

    def greet(hello):
        for device in (up, down, mate, sibling):
            hello(device)
        for dx in range(1, 4):
            hello(dev((x + dx) % 4, y, sz, half))
        hello(dev(x, y, sz, half), crossed)
        expected = 7 + crossed.astype(jnp.int32)
        for j in range(4):
            hello(
                dev(x, j, from_z, from_core),
                jnp.logical_not((j == y) & (from_z == z) & (from_core == core)),
            )
            expected = expected + jnp.logical_not((sz == y) & (z == j) & (half == core)).astype(jnp.int32)
        return expected

    slot = s * 4 + y

    def block(b):
        return pl.ds(b * 80, 80)

    mine = pl.ds(pl.multiple_of(x * 80, 80), 80)

    def to_group(fr):
        return pltpu.make_async_remote_copy(
            src_ref=z_ref.at[fr],
            dst_ref=own_z.at[mine],
            send_sem=s1.at[fr],
            recv_sem=r1.at[x],
            device_id=dev(fr, y, sz, half),
            device_id_type=MESH,
        )

    def lowered_ready(fr):
        stays = uncrossed & (x == fr)

        @pl.when(jnp.logical_not(stays))
        def _():
            to_group(fr).start()

        @pl.when(stays)
        def _():
            own_z[mine, :] = z_ref[fr]

    def weights_ready():
        for load in loads:
            load.wait()
        together = dot_f32(wq_ref[...], wk_ref[...], ((1,), (1,))) * (256.0 ** -0.5 * 1.4426950408889634)
        w_qk[0], w_qk[1] = split(together)
        w_vo[0], w_vo[1] = split(dot_f32(wv_ref[...], wo_ref[...]))

    def three_part(values, weight):
        high, low = split(values)
        total = jnp.dot(high, weight[0], preferred_element_type=F32)
        total = total + jnp.dot(high, weight[1], preferred_element_type=F32)
        return total + jnp.dot(low, weight[0], preferred_element_type=F32)

    def run():
        sent = []
        slot_up = s * 4 + (y + 1) % 4
        slot_down = s * 4 + (y + 3) % 4
        slot_far = s * 4 + (y + 2) % 4
        other = (1 - s) * 4
        mate_own, mate_up = other + y, other + (y + 1) % 4
        mate_down, mate_far = other + (y + 3) % 4, other + (y + 2) % 4

        def remote(src, dst, device, i):
            return pltpu.make_async_remote_copy(
                src_ref=src, dst_ref=dst, send_sem=ss.at[i], recv_sem=rs.at[i],
                device_id=device, device_id_type=MESH,
            )

        own_up, own_down, own_mate, mate_goes_up, mate_goes_down, far_on, far_mate = range(7)

        def push(kind, b, source, device):
            ref = keys.at[source, block(b)]
            copy = remote(ref, ref, device, kind * 4 + b)
            copy.start()
            sent.append(copy)

        def landed(kind, b, source):
            ref = keys.at[source, block(b)]
            remote(ref, ref, sibling, kind * 4 + b).wait_recv()

        gain = gain_ref[...]
        for b in range(4):
            @pl.when(jnp.logical_not(uncrossed & (x == b)))
            def _():
                pltpu.make_async_remote_copy(
                    src_ref=z_ref.at[0],
                    dst_ref=own_z.at[block(b)],
                    send_sem=s1.at[b],
                    recv_sem=r1.at[b],
                    device_id=sibling,
                    device_id_type=MESH,
                ).wait_recv()

            keys[slot, block(b), :] = norm(own_z[block(b)], gain)
            push(own_up, b, slot, up)
            push(own_down, b, slot, down)
            push(own_mate, b, slot, mate)
        def place_query(at, values):
            rows = slice(at, at + 320)
            high, low = split(values[...])
            q_ref[rows, 0:256] = high
            q_ref[rows, 256:512] = low
            q_ref[rows, 512:768] = high

        q_own[...] = three_part(keys[slot], w_qk)
        q_copy = remote(q_own, q_in, sibling, 28)
        q_copy.start()
        sent.append(q_copy)
        place_query(0, q_own)

        best[...] = jnp.full_like(best, -jnp.inf)
        total[...] = jnp.zeros_like(total)
        acc[...] = jnp.zeros_like(acc)

        def product(a, b, dims):
            return lax.dot_general(a, b, (dims, ((), ())), preferred_element_type=F32)

        def prepare(at, source):
            place = slice(at * 320, at * 320 + 320)
            high, low = split(keys[source])
            k_ref[place, 0:256] = high
            k_ref[place, 256:512] = high
            k_ref[place, 512:768] = low

        def attend(start, stop, rows):
            place = slice(start * 320, stop * 320)
            k_hi, k_lo = k_ref[place, 0:256], k_ref[place, 512:768]
            scores = product(q_ref[rows], k_ref[place], ((1,), (1,)))
            old = best[rows]
            new = jnp.maximum(old, jnp.max(scores, axis=1, keepdims=True))
            factor = jnp.exp2(old - new)
            weights = jnp.exp2(scores - new)
            total[rows] = total[rows] * factor + jnp.sum(weights, axis=1, keepdims=True)
            best[rows] = new
            p_hi, p_lo = split(weights)
            along = ((1,), (0,))
            mixed = product(p_hi, k_hi, along) + product(p_hi, k_lo, along) + product(p_lo, k_hi, along)
            acc[rows] = acc[rows] * factor + mixed

        first, second = slice(0, 320), slice(320, 640)

        def forward(b):
            if b < 2:
                landed(own_up, b, slot_down)
                push(far_on, b, slot_down, up)
                landed(own_down, b, slot_up)
            else:
                landed(own_down, b, slot_up)
                push(far_on, b, slot_up, down)
                landed(own_up, b, slot_down)
            landed(own_mate, b, mate_own)
            push(mate_goes_up, b, mate_own, up)
            push(mate_goes_down, b, mate_own, down)

        def far_forward(b):
            landed(far_on, b, slot_far)
            push(far_mate, b, slot_far, mate)

        forward(0)
        prepare(0, slot)
        attend(0, 1, first)
        forward(1)
        q_copy.wait_recv()
        place_query(320, q_in)
        attend(0, 1, second)
        forward(2)
        forward(3)
        prepare(1, slot_down)
        far_forward(0)
        prepare(2, slot_up)
        far_forward(1)
        far_forward(2)
        prepare(3, mate_own)
        far_forward(3)
        prepare(4, slot_far)
        attend(1, 5, second)
        attend(1, 5, first)
        for b in range(4):
            landed(mate_goes_up, b, mate_down)
        prepare(5, mate_down)
        for b in range(4):
            landed(mate_goes_down, b, mate_up)
        prepare(6, mate_up)
        for b in range(4):
            landed(far_mate, b, mate_far)
        prepare(7, mate_far)
        attend(5, 8, second)
        part_stat[0, :, 0:64] = jnp.broadcast_to(best[second], (320, 64))
        part_stat[0, :, 64:128] = jnp.broadcast_to(total[second], (320, 64))
        merge = [
            remote(part_stat.at[0], part_stat.at[1], sibling, 30),
            remote(acc.at[pl.ds(320, 320)], part_acc, sibling, 29),
        ]
        for copy in merge:
            copy.start()
        attend(5, 8, first)
        for copy in merge:
            copy.wait_recv()
        sent.extend(merge)
        other_best = part_stat[1, :, 0:1]
        other_total = part_stat[1, :, 64:65]
        top = jnp.maximum(best[first], other_best)
        mine_f = jnp.exp2(best[first] - top)
        other_f = jnp.exp2(other_best - top)
        whole = total[first] * mine_f + other_total * other_f
        mixed = (acc[first] * mine_f + part_acc[...] * other_f) / whole
        y_out = own_z[...] + three_part(mixed, w_vo)

        backs = []
        for part in range(4):
            for b in range(4):
                start = b * 80 + part * 20
                result[part, b * 20 : b * 20 + 20] = y_out[start : start + 20]
            copy = pltpu.make_async_remote_copy(
                src_ref=result.at[part],
                dst_ref=landing.at[y],
                send_sem=rets.at[part],
                recv_sem=retr.at[y],
                device_id=dev(x, sz, part, half),
                device_id_type=MESH,
            )
            stays = (sz == y) & (z == part) & (half == core)
            backs.append((copy, stays))

            @pl.when(jnp.logical_not(stays))
            def _():
                copy.start()

            @pl.when(stays)
            def _():
                landing[y] = result[part]

        for sy in range(4):
            here = (sy == y) & (from_z == z) & (from_core == core)

            @pl.when(jnp.logical_not(here))
            def _():
                pltpu.make_async_remote_copy(
                    src_ref=result.at[0],
                    dst_ref=landing.at[sy],
                    send_sem=rets.at[0],
                    recv_sem=retr.at[sy],
                    device_id=sibling,
                    device_id_type=MESH,
                ).wait_recv()

            for sx in range(4):
                at = (sx * 4 + sy) * 20
                out_ref[0, at : at + 20, :] = landing[sy, sx * 20 : sx * 20 + 20]

        for fr in range(4):
            @pl.when(jnp.logical_not(uncrossed & (x == fr)))
            def _():
                to_group(fr).wait_send()

        for copy in sent:
            copy.wait_send()
        for copy, stays in backs:
            @pl.when(jnp.logical_not(stays))
            def _():
                copy.wait_send()

    return greet, weights_ready, lowered_ready, run


CONV_SCRATCH = [
    ((4, 2, 160, 128), F32), ((2, 1152, 128), F32), ((2, 384, 128), F32), ((1152, 256), F32),
    ((4, 8, 40, 128), F32), ((3, 4, 10, 56, 128), F32), ((4, 4, 4, 1, 128), F32), ((4, 4, 4, 1, 128), F32),
    ((2, 2, 4, 8, 1, 128), F32), ((2, 2, 4, 8, 1, 128), F32), ((2, 4, 4, 1, 128), F32), ((2, 4, 4, 1, 128), F32),
    ((2, 2, 320, 128), F32), ((2, 2, 320, 128), F32), ((320, 768), BF16), ((320, 768), BF16),
    ((2, 320, 1152), BF16), ((2, 320, 1152), BF16), ((192, 1152), F32), ((192, 1152), F32),
    ((2, 1152, 256), BF16), ((2, 384, 256), BF16), ((1152, 256), BF16), ((1152, 256), BF16),
]
ATTEND_SCRATCH = [
    ((8, 320, 256), F32), ((640, 768), BF16), ((320, 256), F32), ((320, 256), F32),
    ((640, 256), F32), ((640, 1), F32), ((640, 1), F32), ((320, 256), F32), ((2, 320, 128), F32),
    ((4, 80, 256), F32), ((4, 80, 256), F32), ((2560, 768), BF16),
    ((320, 256), F32), ((2, 256, 256), BF16), ((2, 256, 256), BF16),
]
CONV_SEMS = (56, 56)
ATTEND_SEMS = (4, 4, 31, 31, 4, 4)


def encode_kernel(
    video_hbm, space_hbm, time_hbm, down_hbm, wq_hbm, wk_hbm, wv_hbm, wo_hbm, gain_ref, attn_gain_ref, out_ref,
    z_ref, wq_ref, wk_ref, wv_ref, wo_ref, load_sems, *scratch,
):
    c, a = len(CONV_SCRATCH), len(ATTEND_SCRATCH)
    conv_scratch, attend_scratch = scratch[:c], scratch[c : c + a]
    conv_sems, attend_sems = scratch[c + a : c + a + 2], scratch[c + a + 2 :]
    pairs = ((wq_hbm, wq_ref), (wk_hbm, wk_ref), (wv_hbm, wv_ref), (wo_hbm, wo_ref))
    loads = [pltpu.make_async_copy(src, dst, load_sems.at[4 + i]) for i, (src, dst) in enumerate(pairs)]
    greet, weights_ready, lowered_ready, attend = attend_part(
        attn_gain_ref, loads, wq_ref, wk_ref, wv_ref, wo_ref, z_ref, out_ref, *attend_scratch, *attend_sems
    )
    for load in loads:
        load.start()
    finish = conv_part(
        video_hbm, space_hbm, time_hbm, down_hbm, gain_ref, z_ref, *conv_scratch, *conv_sems,
        load_sems, greet, weights_ready, lowered_ready,
    )
    attend()
    finish()


def local(
    video,
    norm_gain,
    space_weight,
    time_weight,
    down_weight,
    attn_gain,
    w_query,
    w_key,
    w_value,
    w_out,
):
    vmem = pl.BlockSpec(memory_space=pltpu.VMEM)
    hbm = pl.BlockSpec(memory_space=pltpu.HBM)
    dma = pltpu.SemaphoreType.DMA
    square = pltpu.VMEM((256, 256), F32)
    return pl.pallas_call(
        encode_kernel,
        out_shape=jax.ShapeDtypeStruct((1, 320, 256), F32),
        in_specs=[hbm] * 8 + [vmem] * 2,
        out_specs=vmem,
        scratch_shapes=[
            pltpu.VMEM((4, 80, 256), F32), square, square, square, square, dma((8,)),
            *[pltpu.VMEM(shape, dtype) for shape, dtype in CONV_SCRATCH + ATTEND_SCRATCH],
            *[dma((count,)) for count in CONV_SEMS + ATTEND_SEMS],
        ],
        compiler_params=pltpu.CompilerParams(
            collective_id=3, has_side_effects=True, vmem_limit_bytes=56 * 2**20
        ),
        name="encode",
    )(
        video, space_weight.reshape(2, 1152, 128), time_weight.reshape(2, 384, 128), down_weight.reshape(1152, 256),
        w_query, w_key, w_value, w_out, norm_gain, attn_gain.reshape(1, 256),
    )


def solution(mesh):
    in_specs = (P("frame", "tile", None, None), P(), P(), P(), P(), P(), P(), P(), P(), P())
    out_specs = P(("frame", "tile"), None, None)
    return jax.shard_map(local, mesh=mesh, in_specs=in_specs, out_specs=out_specs, check_vma=False)
```
